1024 devices in a mesh: gx: 32 (over x_lo, y, core), gy: 32 (over x_hi, z).
Axes of the slice: x: 4 (x_hi: 2, x_lo: 2; x = x_hi * 2 + x_lo), y: 8, z: 16, core: 2. Of those that a mesh axis runs over, the one named last changes fastest.
Arguments:
- velocity: float32 [3, 512, 512, 128], P(None, 'gx', 'gy'), may hold values from -6 to 6
- stress: float32 [6, 512, 512, 128], P(None, 'gx', 'gy'), may hold values from -6 to 6
- buoyancy: float32 [512, 512, 128], P('gx', 'gy'), may hold values from 0.5 to 2
- lame_lambda: float32 [512, 512, 128], P('gx', 'gy'), may hold values from 0.5 to 2
- shear_modulus: float32 [512, 512, 128], P('gx', 'gy'), may hold values from 0.5 to 2
- slot_moment: float32 [32, 32, 6, 64], P('gx', 'gy'), may hold values from -24 to 24
- slot_signal: float32 [32, 32, 64], P('gx', 'gy'), may hold values from 0.5 to 2
- slot_x: int32 [32, 32, 64], P('gx', 'gy'), may hold values from 0 to 15
- slot_y: int32 [32, 32, 64], P('gx', 'gy'), may hold values from 0 to 15
- slot_z: int32 [32, 32, 64], P('gx', 'gy'), may hold values from 0 to 127
- slot_count: int32 [32, 32, 1], P('gx', 'gy'), may hold values from 0 to 64, as said below
Outputs:
- new_velocity: float32 [3, 512, 512, 128], P(None, 'gx', 'gy')
- new_stress: float32 [6, 512, 512, 128], P(None, 'gx', 'gy')
The draws below stay inside these ranges and needn't reach their ends.
Inputs may be any that keep to these rules, and one draw needn't show every extreme that they name: `slot_count`: slots at or beyond a tile's count are unused; at least one tile uses all 64 slots.
All inputs are finite; a program needn't handle non-finite values.
Results may differ from the reference program's by a relative error of at most 0.00005.
Values sent between devices are 32-bit elements; how exact they have to be, the bound alone decides.
A program may use at most 64 MiB of HBM per device.

```python
import math
import jax
import jax.numpy as jnp
from jax import lax

CX = 16
CY = 16
NZ = 128
SLOTS = 64
NX = 512
NY = 512
N_GX = 32
N_GY = 32


def draw_slot_count(key, part):
    key = jax.random.fold_in(key, 11)
    key_one, key_two, key_three = jax.random.split(key, 3)
    first = jax.random.randint(key_one, (N_GX, N_GY, 1), 0, SLOTS + 1)
    second = jax.random.randint(key_two, (N_GX, N_GY, 1), 0, SLOTS + 1)
    product = first * second // SLOTS
    chosen = jax.random.randint(key_three, (), 0, N_GX * N_GY)
    flat = jnp.arange(N_GX * N_GY, dtype=jnp.int32).reshape(N_GX, N_GY, 1)
    return jnp.where(flat == chosen, SLOTS, product).astype(jnp.int32)


def plant(values, own_key, low, high):
    spot = [jax.random.randint(jax.random.fold_in(own_key, axis), (), 0, length) for axis, length in enumerate(values.shape)]
    main_axis = values.shape.index(max(values.shape))
    next_to = spot[:main_axis] + [(spot[main_axis] + 1) % values.shape[main_axis]] + spot[main_axis + 1:]
    return values.at[tuple(spot)].set(low).at[tuple(next_to)].set(high)


def shard_levels(own_key, dims, pieces, smallest, high):
    loudness = 1.0
    for position, blocks in pieces:
        draws = jax.random.uniform(jax.random.fold_in(jax.random.fold_in(own_key, 6), position), (blocks,), jnp.float32, smallest / len(pieces), high / len(pieces))
        loudness = loudness * jnp.repeat(jnp.exp(draws), dims[position] // blocks).reshape((-1,) + (1,) * (len(dims) - 1 - position))
    return loudness


def bell_draw(own_key, shape, scale, reach, cuts=(), held_as=jnp.bfloat16):
    loudness = shard_levels(own_key, shape, cuts, -0.22, 0.18) if cuts else 1.0
    values = jax.random.normal(own_key, shape, jnp.float32) * scale * loudness
    return jnp.minimum(jnp.maximum(values, -reach), reach).astype(held_as)


def setup_inputs(seed: int = 0) -> dict:
    splits = jax.random.split(jax.random.key(seed), 12)
    return {
        "velocity": bell_draw(splits[0], (3, NX, NY, NZ), 1.0, 6.0, ((1, 32), (2, 32)), jnp.float32),
        "stress": bell_draw(splits[1], (6, NX, NY, NZ), 1.0, 6.0, ((1, 32), (2, 32)), jnp.float32),
        "buoyancy": jnp.clip(jnp.exp(math.log(2.0) - 1.3862944 * jax.random.uniform(splits[2], (NX, NY, NZ), jnp.float32) ** shard_levels(splits[2], (NX, NY, NZ), ((0, 32), (1, 32)), -0.2, 0.2)), 0.5, 2.0),
        "lame_lambda": jnp.clip(jnp.exp(math.log(2.0) - 1.3862944 * jax.random.uniform(splits[3], (NX, NY, NZ), jnp.float32) ** shard_levels(splits[3], (NX, NY, NZ), ((0, 32), (1, 32)), -0.2, 0.2)), 0.5, 2.0),
        "shear_modulus": jnp.clip(jnp.exp(math.log(2.0) - 1.3862944 * jax.random.uniform(splits[4], (NX, NY, NZ), jnp.float32) ** shard_levels(splits[4], (NX, NY, NZ), ((0, 32), (1, 32)), -0.2, 0.2)), 0.5, 2.0),
        "slot_moment": bell_draw(splits[5], (N_GX, N_GY, 6, SLOTS), 4.0, 24.0, ((0, 32), (1, 32)), jnp.float32),
        "slot_signal": jnp.clip(jnp.exp(math.log(2.0) - 1.3862944 * jax.random.uniform(splits[6], (N_GX, N_GY, SLOTS), jnp.float32) ** shard_levels(splits[6], (N_GX, N_GY, SLOTS), ((0, 32), (1, 32)), -0.2, 0.2)), 0.5, 2.0),
        "slot_x": plant(jax.random.randint(splits[7], (N_GX, N_GY, SLOTS), 0, CX), jax.random.fold_in(splits[7], 1), 0, CX - 1).astype(jnp.int32),
        "slot_y": plant(jax.random.randint(splits[8], (N_GX, N_GY, SLOTS), 0, CY), jax.random.fold_in(splits[8], 1), 0, CY - 1).astype(jnp.int32),
        "slot_z": plant(jax.random.randint(splits[9], (N_GX, N_GY, SLOTS), 0, NZ), jax.random.fold_in(splits[9], 1), 0, NZ - 1).astype(jnp.int32),
        "slot_count": draw_slot_count(jax.random.fold_in(splits[11], 71), 0),
    }


coef_one = 9.0 / 8.0
coef_two = -1.0 / 24.0
time_step = 0.1
pairs = ((0, 3, 4), (3, 1, 5), (4, 5, 2))


def derive(padded, axis, forward):
    count = padded.shape[axis] - 4

    def part(low):
        return lax.slice_in_dim(padded, low, low + count, axis=axis)

    if forward:
        value = coef_one * (part(3) - part(2)) + coef_two * (part(4) - part(1))
    else:
        value = coef_one * (part(2) - part(1)) + coef_two * (part(3) - part(0))
    for other in range(3):
        if other != axis:
            value = lax.slice_in_dim(value, 2, value.shape[other] - 2, axis=other)
    return value


def velocity_step(velocity, padded_stress, buoyancy, force):
    sxx, syy, szz, sxy, sxz, syz = [padded_stress[k] for k in range(6)]
    accel_x = derive(sxx, 0, True) + derive(sxy, 1, False) + derive(sxz, 2, False)
    accel_y = derive(sxy, 0, False) + derive(syy, 1, True) + derive(syz, 2, False)
    accel_z = derive(sxz, 0, False) + derive(syz, 1, False) + derive(szz, 2, True)
    accel = jnp.stack([accel_x, accel_y, accel_z])
    return velocity + time_step * buoyancy[None] * (accel + force)


def stress_step(stress, padded_vel, lame_lambda, shear_modulus):
    vel_x, vel_y, vel_z = padded_vel[0], padded_vel[1], padded_vel[2]
    exx = derive(vel_x, 0, False)
    eyy = derive(vel_y, 1, False)
    ezz = derive(vel_z, 2, False)
    trace = exx + eyy + ezz
    sxx = stress[0] + time_step * (lame_lambda * trace + 2.0 * shear_modulus * exx)
    syy = stress[1] + time_step * (lame_lambda * trace + 2.0 * shear_modulus * eyy)
    szz = stress[2] + time_step * (lame_lambda * trace + 2.0 * shear_modulus * ezz)
    sxy = stress[3] + time_step * shear_modulus * (derive(vel_x, 1, True) + derive(vel_y, 0, True))
    sxz = stress[4] + time_step * shear_modulus * (derive(vel_x, 2, True) + derive(vel_z, 0, True))
    syz = stress[5] + time_step * shear_modulus * (derive(vel_y, 2, True) + derive(vel_z, 1, True))
    return jnp.stack([sxx, syy, szz, sxy, sxz, syz])


def stencils():
    deriv = jnp.array([1.0 / 24.0, -9.0 / 8.0, 9.0 / 8.0, -1.0 / 24.0], jnp.float32)
    weight = jnp.array([-1.0 / 16.0, 9.0 / 16.0, 9.0 / 16.0, -1.0 / 16.0], jnp.float32)
    along_x = deriv[:, None, None] * weight[None, :, None] * weight[None, None, :]
    along_y = weight[:, None, None] * deriv[None, :, None] * weight[None, None, :]
    along_z = weight[:, None, None] * weight[None, :, None] * deriv[None, None, :]
    return jnp.stack([along_x, along_y, along_z])


def reference(velocity, stress, buoyancy, lame_lambda, shear_modulus, slot_moment, slot_signal, slot_x, slot_y, slot_z, slot_count):
    live = (jnp.arange(SLOTS, dtype=jnp.int32)[None, None, :] < slot_count).astype(jnp.float32)
    scaled = slot_signal * live
    amp = jnp.stack([jnp.stack([-slot_moment[:, :, pairs[i][j], :] * scaled for j in range(3)], -1) for i in range(3)], -2)
    amp = amp.reshape(-1, 3, 3)
    gpos_x = (slot_x + CX * jnp.arange(N_GX, dtype=jnp.int32)[:, None, None]).reshape(-1).astype(jnp.int32)
    gpos_y = (slot_y + CY * jnp.arange(N_GY, dtype=jnp.int32)[None, :, None]).reshape(-1).astype(jnp.int32)
    gpos_z = slot_z.reshape(-1).astype(jnp.int32)
    weights = jnp.einsum("sij,jabc->siabc", amp, stencils())
    offs = jnp.arange(4, dtype=jnp.int32) + 1
    comp = jnp.arange(3, dtype=jnp.int32)[None, :, None, None, None]
    index_x = gpos_x[:, None, None, None, None] + offs[None, None, :, None, None]
    index_y = gpos_y[:, None, None, None, None] + offs[None, None, None, :, None]
    index_z = gpos_z[:, None, None, None, None] + offs[None, None, None, None, :]
    shape = weights.shape
    total = jnp.zeros((3, NX + 4, NY + 4, NZ + 4), jnp.float32)
    total = total.at[jnp.broadcast_to(comp, shape), jnp.broadcast_to(index_x, shape), jnp.broadcast_to(index_y, shape), jnp.broadcast_to(index_z, shape)].add(weights)
    force = total[:, 2:NX + 2, 2:NY + 2, 2:NZ + 2]
    padded_stress = jnp.pad(stress, ((0, 0), (2, 2), (2, 2), (2, 2)))
    new_velocity = velocity_step(velocity, padded_stress, buoyancy, force)
    padded_vel = jnp.pad(new_velocity, ((0, 0), (2, 2), (2, 2), (2, 2)))
    new_stress = stress_step(stress, padded_vel, lame_lambda, shear_modulus)
    return new_velocity, new_stress
```

```python
import functools
import jax
import jax.numpy as jnp
from jax import lax
from jax.sharding import PartitionSpec as P
import jax.experimental.pallas as pl
import jax.experimental.pallas.tpu as pltpu

MESH = pl.DeviceIdType.MESH
F32 = jnp.float32
BF16 = jnp.bfloat16

c1 = 9.0 / 8.0
c2 = -1.0 / 24.0
time_step = 0.1
d_table = (1.0, -27.0, 27.0, -1.0)
w_table = (-1.0, 9.0, 9.0, -1.0)
unscale = 1.0 / (16.0 * 16.0 * 24.0)
pairs = ((0, 3, 4), (3, 1, 5), (4, 5, 2))
neighbours = ((-1, -1), (-1, 0), (-1, 1), (0, -1), (0, 1), (1, -1), (1, 0), (1, 1))


def lookup(offset, table):
    value = jnp.where(offset == 3, table[3], 0.0)
    for k in (2, 1, 0):
        value = jnp.where(offset == k, table[k], value)
    return value


def halves(low, high):
    lane = lax.broadcasted_iota(jnp.int32, (1, 128), 1)
    return jnp.where(lane < 64, low, high)


def stencil(length, start, position, table):
    cell = lax.broadcasted_iota(jnp.int32, (length, 128), 0) + start
    return lookup(cell - position + 1, table)


def depth_weights(pz):
    table = [halves(w, d) for w, d in zip(w_table, d_table)]
    weights = stencil(128, 0, pz, table).astype(BF16)
    return jnp.concatenate([weights, weights], axis=1)


def split(value):
    high = value.astype(BF16)
    low = (value - high.astype(F32)).astype(BF16)
    return jnp.concatenate([high, low], axis=1)


def cell_weights(slots, start_x, count_x, start_y, count_y, shift, y_major=False):
    px = slots[6:7, :].astype(jnp.int32) + shift[0]
    py = slots[7:8, :].astype(jnp.int32) + shift[1]
    mixed = [halves(d, w) for w, d in zip(w_table, d_table)]
    xa = stencil(count_x, start_x, px, mixed)
    xb = stencil(count_x, start_x, px, w_table)
    ya = stencil(count_y, start_y, py, w_table)
    yb = stencil(count_y, start_y, py, d_table)
    parts = []
    for i in range(3):
        p = slots[i : i + 1, :]
        q = slots[3 + i : 4 + i, :]
        if y_major:
            one, two = p * ya, q * yb
            rows = [one[k : k + 1, :] * xa + two[k : k + 1, :] * xb for k in range(count_y)]
        else:
            one, two = p * xa, q * xb
            rows = [one[k : k + 1, :] * ya + two[k : k + 1, :] * yb for k in range(count_x)]
        parts += rows
    return split(jnp.concatenate(parts, axis=0))


def matmul(left, right):
    return lax.dot_general(left, right, (((1,), (1,)), ((), ())), preferred_element_type=F32)


def diff(m2, m1, f, p1):
    return c1 * (f - m1) + c2 * (p1 - m2)


def along_y(f, low2, low1, high1, high2, forward):
    iy = lax.broadcasted_iota(jnp.int32, f.shape, 0)
    m1 = jnp.where(iy == 0, low1, pltpu.roll(f, 1, 0))
    p1 = jnp.where(iy == 15, high1, pltpu.roll(f, 15, 0))
    if forward:
        p2 = jnp.where(iy == 15, high2, jnp.where(iy == 14, high1, pltpu.roll(f, 14, 0)))
        return diff(m1, f, p1, p2)
    m2 = jnp.where(iy == 0, low2, jnp.where(iy == 1, low1, pltpu.roll(f, 2, 0)))
    return diff(m2, m1, f, p1)


def along_z(f, forward):
    iz = lax.broadcasted_iota(jnp.int32, f.shape, 1)
    m1 = jnp.where(iz < 1, 0.0, pltpu.roll(f, 1, 1))
    p1 = jnp.where(iz > 126, 0.0, pltpu.roll(f, 127, 1))
    if forward:
        p2 = jnp.where(iz > 125, 0.0, pltpu.roll(f, 126, 1))
        return diff(m1, f, p1, p2)
    m2 = jnp.where(iz < 2, 0.0, pltpu.roll(f, 2, 1))
    return diff(m2, m1, f, p1)


def kernel(
    nx, ny,
    v_in, s_in, b_in, l_in, m_in, mom_in, sig_in, px_in, py_in, pz_in, cnt_in,
    nv, ns,
    vel, st, buo, lam, mu, mom, sig, px, py, pz,
    slots, slots_from, ysend, ylow, yhigh, force, u, uysend, uylow, uyhigh,
    load_sem, send_sem, recv_sem,
):
    gx, gy = lax.axis_index("gx"), lax.axis_index("gy")

    def there(dx, dy):
        ok = True
        for at, step, count in ((gx, dx, nx), (gy, dy, ny)):
            if step:
                ok = ok & (at > 0) if step < 0 else ok & (at < count - 1)
        return ok

    barrier = pltpu.get_barrier_semaphore()
    expected = 0
    for dx, dy in neighbours:
        expected = expected + there(dx, dy).astype(jnp.int32)

        @pl.when(there(dx, dy))
        def _():
            pl.semaphore_signal(barrier, inc=1, device_id=(gx + dx, gy + dy), device_id_type=MESH)

    loads = {}
    for k, (name, src, dst) in enumerate((
        ("mom", mom_in, mom), ("sig", sig_in, sig), ("px", px_in, px), ("py", py_in, py),
        ("pz", pz_in, pz),
        ("st", s_in, st.at[:, 2:18]), ("vel", v_in, vel), ("buo", b_in, buo),
        ("lam", l_in, lam), ("mu", m_in, mu),
    )):
        loads[name] = pltpu.make_async_copy(src, dst, load_sem.at[k])
        loads[name].start()

    @pl.when(gx == 0)
    def _():
        st[:, 0:2] = jnp.zeros((6, 2, 16, 128), F32)
        u[:, 0:2] = jnp.zeros((3, 2, 16, 128), F32)

    @pl.when(gx == nx - 1)
    def _():
        st[:, 18:20] = jnp.zeros((6, 2, 16, 128), F32)
        u[:, 18:20] = jnp.zeros((3, 2, 16, 128), F32)

    @pl.when(gy == 0)
    def _():
        ylow[...] = jnp.zeros((5, 16, 128), F32)
        uylow[...] = jnp.zeros((4, 16, 128), F32)

    @pl.when(gy == ny - 1)
    def _():
        yhigh[...] = jnp.zeros((4, 16, 128), F32)
        uyhigh[...] = jnp.zeros((5, 16, 128), F32)

    for k, (dx, dy) in enumerate(neighbours):
        @pl.when(jnp.logical_not(there(dx, dy)))
        def _():
            slots_from[k] = jnp.zeros((16, 128), F32)

    for name in ("mom", "sig", "px", "py", "pz"):
        loads[name].wait()
    lane = lax.broadcasted_iota(jnp.int32, (1, 64), 1)
    live = (lane < cnt_in[0, 0, 0]).astype(F32)
    scaled = sig[0] * live * (-unscale)
    amp = [mom[0, r] * scaled for r in range(6)]
    nothing = jnp.zeros((1, 64), F32)
    rows = [jnp.concatenate([amp[pairs[i][0]], amp[pairs[i][2]]], axis=1) for i in range(3)]
    rows += [jnp.concatenate([amp[pairs[i][1]], nothing], axis=1) for i in range(3)]
    for ref in (px, py, pz):
        at = ref[0].astype(F32)
        rows.append(jnp.concatenate([at, at], axis=1))
    for r, row in enumerate(rows):
        slots[r : r + 1, :] = row
    slots[9:16, :] = jnp.zeros((7, 128), F32)

    def remote(k, src, dst, dx, dy):
        return pltpu.make_async_remote_copy(
            src_ref=src, dst_ref=dst, send_sem=send_sem.at[k], recv_sem=recv_sem.at[k],
            device_id=(gx + dx, gy + dy), device_id_type=MESH,
        )

    first = []
    for k, (dx, dy) in enumerate(neighbours):
        first.append((remote(k, slots, slots_from.at[7 - k], dx, dy), dx, dy))
    first_x = [
        (remote(8, s_in.at[0:1, 15:16], st.at[0:1, 1:2], 1, 0), 1, 0),
        (remote(9, s_in.at[3:5, 14:16], st.at[3:5, 0:2], 1, 0), 1, 0),
        (remote(10, s_in.at[0:1, 0:2], st.at[0:1, 18:20], -1, 0), -1, 0),
        (remote(11, s_in.at[3:5, 0:1], st.at[3:5, 18:19], -1, 0), -1, 0),
    ]
    first_y = [
        (remote(12, ysend.at[0:5], ylow, 0, 1), 0, 1),
        (remote(13, ysend.at[5:9], yhigh, 0, -1), 0, -1),
    ]
    second_x = [
        (remote(14, u.at[0:1, 16:18], u.at[0:1, 0:2], 1, 0), 1, 0),
        (remote(15, u.at[1:3, 17:18], u.at[1:3, 1:2], 1, 0), 1, 0),
        (remote(16, u.at[0:1, 2:3], u.at[0:1, 18:19], -1, 0), -1, 0),
        (remote(17, u.at[1:3, 2:4], u.at[1:3, 18:20], -1, 0), -1, 0),
    ]
    second_y = [
        (remote(18, uysend.at[0:4], uylow, 0, 1), 0, 1),
        (remote(19, uysend.at[4:9], uyhigh, 0, -1), 0, -1),
    ]

    def start(copies):
        for copy, dx, dy in copies:
            @pl.when(there(dx, dy))
            def _():
                copy.start()

    def arrive(copies):
        for copy, dx, dy in copies:
            @pl.when(there(-dx, -dy))
            def _():
                copy.wait_recv()

    def sent(copies):
        for copy, dx, dy in copies:
            @pl.when(there(dx, dy))
            def _():
                copy.wait_send()

    loads["st"].wait()
    for k, (f, y) in enumerate(((3, 14), (3, 15), (1, 15), (5, 14), (5, 15), (3, 0), (1, 0), (1, 1), (5, 0))):
        ysend[k] = st[f, 2:18, y, :]

    pl.semaphore_wait(barrier, expected)
    start(first_y)
    start(first)
    start(first_x)

    own = matmul(cell_weights(slots[...], 0, 16, 0, 16, (0, 0)), depth_weights(slots[8:9, :].astype(jnp.int32)))
    force[...] = own.reshape(3, 16, 16, 128)

    arrive(first)
    near = {n: slots_from[k] for k, n in enumerate(neighbours)}
    deep = {n: depth_weights(near[n][8:9, :].astype(jnp.int32)) for n in neighbours}
    for dx, start_x, count_x in ((-1, 0, 2), (1, 15, 1)):
        total = 0.0
        for dy in (-1, 0, 1):
            n = (dx, dy)
            total = total + matmul(cell_weights(near[n], start_x, count_x, 0, 16, (16 * dx, 16 * dy)), deep[n])
        force[:, start_x : start_x + count_x] += total.reshape(3, count_x, 16, 128)
    for dy, start_y, count_y in ((-1, 0, 2), (1, 15, 1)):
        n = (0, dy)
        got = matmul(cell_weights(near[n], 0, 16, start_y, count_y, (0, 16 * dy), True), deep[n])
        for i in range(3):
            for y in range(count_y):
                r = (i * count_y + y) * 16
                force[i, :, start_y + y, :] += got[r : r + 16, :]

    loads["vel"].wait()
    loads["buo"].wait()
    arrive(first_x)
    arrive(first_y)

    def velocity_plane(x, _):
        p = x + 2

        def low(k):
            return ylow[k, pl.ds(x, 1), :]

        def high(k):
            return yhigh[k, pl.ds(x, 1), :]

        sxy, syy, szz, sxz, syz = st[3, p], st[1, p], st[2, p], st[4, p], st[5, p]
        ax = diff(st[0, p - 1], st[0, p], st[0, p + 1], st[0, p + 2])
        ax += along_y(sxy, low(0), low(1), high(0), None, False) + along_z(sxz, False)
        ay = diff(st[3, p - 2], st[3, p - 1], sxy, st[3, p + 1])
        ay += along_y(syy, None, low(2), high(1), high(2), True) + along_z(syz, False)
        az = diff(st[4, p - 2], st[4, p - 1], sxz, st[4, p + 1])
        az += along_y(syz, low(3), low(4), high(3), None, False) + along_z(szz, True)
        scale = time_step * buo[x]
        nx = vel[0, x] + scale * (ax + force[0, x])
        u[0, p] = nx
        nv[0, x] = nx
        ny = vel[1, x] + scale * (ay + force[1, x])
        u[1, p] = ny
        nv[1, x] = ny
        nz = vel[2, x] + scale * (az + force[2, x])
        u[2, p] = nz
        nv[2, x] = nz
        return 0

    lax.fori_loop(0, 16, velocity_plane, 0)
    for k, (f, y) in enumerate(((0, 15), (1, 14), (1, 15), (2, 15), (0, 0), (0, 1), (1, 0), (2, 0), (2, 1))):
        uysend[k] = u[f, 2:18, y, :]
    start(second_y)
    start(second_x)

    loads["lam"].wait()
    loads["mu"].wait()
    arrive(second_x)
    arrive(second_y)

    def stress_plane(x, _):
        p = x + 2

        def low(k):
            return uylow[k, pl.ds(x, 1), :]

        def high(k):
            return uyhigh[k, pl.ds(x, 1), :]

        ux, uy, uz = u[0, p], u[1, p], u[2, p]
        exx = diff(u[0, p - 2], u[0, p - 1], ux, u[0, p + 1])
        eyy = along_y(uy, low(1), low(2), high(2), None, False)
        ezz = along_z(uz, False)
        two = (2.0 * time_step) * mu[x]
        press = time_step * lam[x] * (exx + eyy + ezz)
        shear = time_step * mu[x]
        ns[0, x] = st[0, p] + (press + two * exx)
        ns[1, x] = st[1, p] + (press + two * eyy)
        ns[2, x] = st[2, p] + (press + two * ezz)
        ns[3, x] = st[3, p] + shear * (
            along_y(ux, None, low(0), high(0), high(1), True)
            + diff(u[1, p - 1], uy, u[1, p + 1], u[1, p + 2])
        )
        ns[4, x] = st[4, p] + shear * (along_z(ux, True) + diff(u[2, p - 1], uz, u[2, p + 1], u[2, p + 2]))
        ns[5, x] = st[5, p] + shear * (along_z(uy, True) + along_y(uz, None, low(3), high(3), high(4), True))
        return 0

    lax.fori_loop(0, 16, stress_plane, 0)
    for copies in (first, first_x, first_y, second_x, second_y):
        sent(copies)


def store(v, s, v_out, s_out, sem):
    copies = [pltpu.make_async_copy(v, v_out, sem.at[0]), pltpu.make_async_copy(s, s_out, sem.at[1])]
    for copy in copies:
        copy.start()
    for copy in copies:
        copy.wait()


def local(velocity, stress, buoyancy, lame_lambda, shear_modulus, moment, signal, sx, sy, sz, count, *, nx, ny):
    hbm = pl.BlockSpec(memory_space=pltpu.HBM)
    on_chip = pl.BlockSpec(memory_space=pltpu.VMEM)
    vmem = pltpu.VMEM
    keep = functools.partial(pltpu.with_memory_space_constraint, memory_space=pltpu.VMEM)
    leave = functools.partial(pltpu.with_memory_space_constraint, memory_space=pltpu.HBM)
    args = (velocity, stress, buoyancy, lame_lambda, shear_modulus, jnp.transpose(moment, (0, 2, 1, 3)), signal, sx, sy, sz)
    done = pl.pallas_call(
        functools.partial(kernel, nx, ny),
        out_shape=(vmem(velocity.shape, F32), vmem(stress.shape, F32)),
        in_specs=[hbm] * 10 + [pl.BlockSpec(memory_space=pltpu.SMEM)],
        out_specs=(on_chip, on_chip),
        scratch_shapes=[
            vmem((3, 16, 16, 128), F32),
            vmem((6, 20, 16, 128), F32),
            vmem((16, 16, 128), F32),
            vmem((16, 16, 128), F32),
            vmem((16, 16, 128), F32),
            vmem((1, 6, 1, 64), F32),
            vmem((1, 1, 64), F32),
            vmem((1, 1, 64), jnp.int32),
            vmem((1, 1, 64), jnp.int32),
            vmem((1, 1, 64), jnp.int32),
            vmem((16, 128), F32),
            vmem((8, 16, 128), F32),
            vmem((9, 16, 128), F32),
            vmem((5, 16, 128), F32),
            vmem((4, 16, 128), F32),
            vmem((3, 16, 16, 128), F32),
            vmem((3, 20, 16, 128), F32),
            vmem((9, 16, 128), F32),
            vmem((4, 16, 128), F32),
            vmem((5, 16, 128), F32),
            pltpu.SemaphoreType.DMA((11,)),
            pltpu.SemaphoreType.DMA((20,)),
            pltpu.SemaphoreType.DMA((20,)),
        ],
        compiler_params=pltpu.CompilerParams(
            collective_id=0, has_side_effects=True, vmem_limit_bytes=48 * 1024 * 1024
        ),
        name="elastic_step",
    )(*map(leave, args), count)
    return pl.pallas_call(
        store,
        out_shape=(pltpu.HBM(velocity.shape, F32), pltpu.HBM(stress.shape, F32)),
        in_specs=[on_chip] * 2,
        out_specs=(hbm, hbm),
        scratch_shapes=[pltpu.SemaphoreType.DMA((2,))],
        name="store_fields",
    )(*map(keep, done))


def solution(mesh):
    field = P(None, "gx", "gy", None)
    cells = P("gx", "gy", None)
    in_specs = (field, field, cells, cells, cells, P("gx", "gy", None, None)) + (cells,) * 5
    step = functools.partial(local, nx=mesh.shape["gx"], ny=mesh.shape["gy"])
    return jax.shard_map(step, mesh=mesh, in_specs=in_specs, out_specs=(field, field), check_vma=False)
```

```python
import functools
import jax
import jax.numpy as jnp
from jax import lax
from jax.sharding import PartitionSpec as P
import jax.experimental.pallas as pl
import jax.experimental.pallas.tpu as pltpu

MESH = pl.DeviceIdType.MESH
F32 = jnp.float32
BF16 = jnp.bfloat16

c1 = 9.0 / 8.0
c2 = -1.0 / 24.0
time_step = 0.1
d_table = (1.0, -27.0, 27.0, -1.0)
w_table = (-1.0, 9.0, 9.0, -1.0)
unscale = 1.0 / (16.0 * 16.0 * 24.0)
pairs = ((0, 3, 4), (3, 1, 5), (4, 5, 2))
neighbours = ((-1, -1), (-1, 0), (-1, 1), (0, -1), (0, 1), (1, -1), (1, 0), (1, 1))


stress_of_p = (("n", 15), ("t", 14), ("t", 15), ("r", 14), ("r", 15))
stress_of_q = (("n", 0), ("n", 1), ("t", 0), ("r", 0))
speed_of_p = (("n", 14), ("n", 15), ("t", 15), ("r", 15))
speed_of_q = (("n", 0), ("t", 0), ("t", 1), ("r", 0), ("r", 1))
component = ({"n": 0, "t": 1, "r": 2}, {"n": 1, "t": 0, "r": 2})
field = ({"n": 0, "t": 3, "r": 4}, {"n": 1, "t": 3, "r": 5})
role = tuple({c: r for r, c in names.items()} for names in component)
head = 8
order = ((0, 1), (1, 1), (-1, 1), (1, 0), (-1, 0), (1, -1), (-1, -1), (0, -1))


def give(get, upward):
    if upward:
        return {
            ("n", 0): lambda: -c2 * get("n", 15),
            ("t", 0): lambda: -c1 * get("t", 15) - c2 * get("t", 14),
            ("t", 1): lambda: -c2 * get("t", 15),
            ("r", 0): lambda: -c1 * get("r", 15) - c2 * get("r", 14),
            ("r", 1): lambda: -c2 * get("r", 15),
        }
    return {
        ("n", 14): lambda: c2 * get("n", 0),
        ("n", 15): lambda: c1 * get("n", 0) + c2 * get("n", 1),
        ("t", 15): lambda: c2 * get("t", 0),
        ("r", 15): lambda: c2 * get("r", 0),
    }


def corner_cells(sx, sy):
    cells = []
    for axis, (across, along) in enumerate(((sx, sy), (sy, sx))):
        other = 1 - axis
        for name, at in speed_of_p if across < 0 else speed_of_q:
            part = role[other][component[axis][name]]
            for what, index in stress_of_p if along < 0 else stress_of_q:
                if what == part:
                    cell = (field[other][what], at, index) if axis == 0 else (field[other][what], index, at)
                    if cell not in cells:
                        cells.append(cell)
    return cells


def lookup(offset, table):
    value = jnp.where(offset == 3, table[3], 0.0)
    for k in (2, 1, 0):
        value = jnp.where(offset == k, table[k], value)
    return value


def halves(low, high):
    lane = lax.broadcasted_iota(jnp.int32, (1, 128), 1)
    return jnp.where(lane < 64, low, high)


def stencil(length, start, position, table):
    cell = lax.broadcasted_iota(jnp.int32, (length, 128), 0) + start
    return lookup(cell - position + 1, table)


def unpack(rows):
    p = [rows[i : i + 1, :] for i in range(3)]
    mixed = [rows[3 + i : 4 + i, :] for i in range(3)]
    q = [halves(row, 0.0) for row in mixed]
    at = [halves(pltpu.roll(row, 64, 1), row).astype(jnp.int32) for row in mixed]
    return p, q, at


def depth_weights(pz):
    table = [halves(w, d) for w, d in zip(w_table, d_table)]
    weights = stencil(128, 0, pz, table).astype(BF16)
    return jnp.concatenate([weights, weights], axis=1)


def spread(tile, shift, pieces):
    p, q, (px, py, pz) = tile
    mixed = [halves(d, w) for w, d in zip(w_table, d_table)]
    position = (px + 16 * shift[0], py + 16 * shift[1])
    tables = ((mixed, w_table), (w_table, d_table))
    rows = []
    for axis, layers, start, count in pieces:
        one = [stencil(len(layers), layers[0], position[axis], table) for table in tables[axis]]
        two = [stencil(count, start, position[1 - axis], table) for table in tables[1 - axis]]
        for i in range(3):
            first, second = p[i] * one[0], q[i] * one[1]
            for k in range(len(layers)):
                rows.append(first[k : k + 1, :] * two[0] + second[k : k + 1, :] * two[1])
    value = jnp.concatenate(rows, axis=0)
    high = value.astype(BF16)
    low = (value - high.astype(F32)).astype(BF16)
    result = lax.dot_general(
        jnp.concatenate([high, low], axis=1), depth_weights(pz), (((1,), (1,)), ((), ())),
        preferred_element_type=F32,
    )
    parts, at = [], 0
    for axis, layers, start, count in pieces:
        size = 3 * len(layers) * count
        parts.append(result[at : at + size])
        at += size
    return parts


def diff(m2, m1, f, p1):
    return c1 * (f - m1) + c2 * (p1 - m2)


def along_y(f, low2, low1, high1, high2, forward):
    iy = lax.broadcasted_iota(jnp.int32, f.shape, 0)
    m1 = jnp.where(iy == 0, low1, pltpu.roll(f, 1, 0))
    p1 = jnp.where(iy == 15, high1, pltpu.roll(f, 15, 0))
    if forward:
        p2 = jnp.where(iy == 15, high2, jnp.where(iy == 14, high1, pltpu.roll(f, 14, 0)))
        return diff(m1, f, p1, p2)
    m2 = jnp.where(iy == 0, low2, jnp.where(iy == 1, low1, pltpu.roll(f, 2, 0)))
    return diff(m2, m1, f, p1)


def along_z(f, forward):
    iz = lax.broadcasted_iota(jnp.int32, f.shape, 1)
    m1 = jnp.where(iz < 1, 0.0, pltpu.roll(f, 1, 1))
    p1 = jnp.where(iz > 126, 0.0, pltpu.roll(f, 127, 1))
    if forward:
        p2 = jnp.where(iz > 125, 0.0, pltpu.roll(f, 126, 1))
        return diff(m1, f, p1, p2)
    m2 = jnp.where(iz < 2, 0.0, pltpu.roll(f, 2, 1))
    return diff(m2, m1, f, p1)


def planes(plane):
    def group(i, _):
        for k in range(4):
            plane(i * 4 + k)
        return 0

    lax.fori_loop(0, 4, group, 0)


def kernel(
    nx, ny,
    v_in, s_in, b_in, l_in, m_in, mom_in, sig_in, px_in, py_in, pz_in, cnt_in,
    nv, ns,
    vel, st, buo, lam, mu, mom, sig, px, py, pz,
    force, u, forces, face_out, face_in, speed_out, speed_in, corner_out, corner_in,
    load_sem, send_sem, recv_sem,
):
    gx, gy = lax.axis_index("gx"), lax.axis_index("gy")

    def there(dx, dy):
        ok = True
        for at, step, count in ((gx, dx, nx), (gy, dy, ny)):
            if step:
                ok = ok & (at > 0) if step < 0 else ok & (at < count - 1)
        return ok

    barrier = pltpu.get_barrier_semaphore()
    expected = 0
    for dx, dy in neighbours:
        expected = expected + there(dx, dy).astype(jnp.int32)

        @pl.when(there(dx, dy))
        def _():
            pl.semaphore_signal(barrier, inc=1, device_id=(gx + dx, gy + dy), device_id_type=MESH)

    loads = {}
    for k, (name, src, dst) in enumerate((
        ("mom", mom_in, mom), ("sig", sig_in, sig), ("px", px_in, px), ("py", py_in, py),
        ("pz", pz_in, pz),
        ("st", s_in, st.at[:, 2:18]), ("vel", v_in, vel), ("buo", b_in, buo),
        ("lam", l_in, lam), ("mu", m_in, mu),
    )):
        loads[name] = pltpu.make_async_copy(src, dst, load_sem.at[k])
        loads[name].start()

    sides = ((-1, 0), (1, 0), (0, -1), (0, 1))
    corners = ((-1, -1), (-1, 1), (1, -1), (1, 1))
    lists = {n: corner_cells(*n) for n in corners}

    for f in (0, 3, 4):
        st[f, 0:2] = jnp.zeros((2, 16, 128), F32)
        st[f, 18:20] = jnp.zeros((2, 16, 128), F32)
    forces[...] = jnp.zeros((8, 3, 2, 16, 128), F32)
    for k, n in enumerate(sides):
        @pl.when(jnp.logical_not(there(*n)))
        def _():
            face_in[k] = jnp.zeros((120, 128), F32)
            speed_in[k] = jnp.zeros((5, 16, 128), F32)

    for k, n in enumerate(corners):
        @pl.when(jnp.logical_not(there(*n)))
        def _():
            corner_in[k] = jnp.zeros((24, 128), F32)

    for name in ("mom", "sig", "px", "py", "pz"):
        loads[name].wait()
    lane = lax.broadcasted_iota(jnp.int32, (1, 64), 1)
    live = (lane < cnt_in[0, 0, 0]).astype(F32)
    scaled = sig[0] * live * (-unscale)
    amp = [mom[0, r] * scaled for r in range(6)]
    rows = [jnp.concatenate([amp[pairs[i][0]], amp[pairs[i][2]]], axis=1) for i in range(3)]
    for i, ref in enumerate((px, py, pz)):
        rows.append(jnp.concatenate([amp[pairs[i][1]], ref[0].astype(F32)], axis=1))
    own_rows = jnp.concatenate(rows, axis=0)
    for k in range(4):
        face_out[k, 0:6, :] = own_rows
        face_out[k, 6:8, :] = jnp.zeros((2, 128), F32)
        corner_out[k, 0:6, :] = own_rows

    def remote(k, src, dst, n):
        return pltpu.make_async_remote_copy(
            src_ref=src, dst_ref=dst, send_sem=send_sem.at[k], recv_sem=recv_sem.at[k],
            device_id=(gx + n[0], gy + n[1]), device_id_type=MESH,
        )

    copies = {}
    for k, n in enumerate(sides):
        upward = k % 2 == 1
        size = head + 16 * (len(stress_of_p if upward else stress_of_q) + 2)
        count = len(speed_of_p if upward else speed_of_q)
        back = (-n[0], -n[1])
        copies["face", back] = remote(k, face_out.at[k, 0:size], face_in.at[k ^ 1, 0:size], n)
        copies["speed", back] = remote(4 + k, speed_out.at[k, 0:count], speed_in.at[k ^ 1, 0:count], n)
    for k, n in enumerate(corners):
        back = (-n[0], -n[1])
        size = -(-(6 + len(lists[back])) // 8) * 8
        copies["corner", back] = remote(8 + k, corner_out.at[k, 0:size], corner_in.at[3 - k, 0:size], n)

    def start(kind):
        for (what, back), copy in copies.items():
            if what == kind:
                @pl.when(there(-back[0], -back[1]))
                def _():
                    copy.start()

    def arrive(kind, n):
        @pl.when(there(*n))
        def _():
            copies[kind, n].wait_recv()

    def layer(ref, axis, f, at):
        return ref[f, at + 2] if axis == 0 else ref[f, 2:18, at, :]

    loads["st"].wait()
    loads["buo"].wait()
    for k in range(4):
        axis, upward = k // 2, k % 2 == 1
        at = head
        for name, index in stress_of_p if upward else stress_of_q:
            face_out[k, at : at + 16, :] = layer(st, axis, field[axis][name], index)
            at += 16
        for index in (14, 15) if upward else (0, 1):
            face_out[k, at : at + 16, :] = buo[index] if axis == 0 else buo[:, index, :]
            at += 16
    for k, n in enumerate(corners):
        for r, (f, x, y) in enumerate(lists[-n[0], -n[1]]):
            corner_out[k, 6 + r : 7 + r, :] = st[f, 2 + x, y : y + 1, :]
        if 6 + len(lists[-n[0], -n[1]]) > 16:
            corner_out[k, 6 + len(lists[-n[0], -n[1]]) : 24, :] = jnp.zeros((18 - len(lists[-n[0], -n[1]]), 128), F32)

    pl.semaphore_wait(barrier, expected)
    start("face")
    start("corner")

    me = unpack(own_rows)
    force[...] = spread(me, (0, 0), [(0, tuple(range(16)), 0, 16)])[0].reshape(3, 16, 16, 128)
    loads["vel"].wait()

    def velocity_plane(x):
        p = x + 2
        sxy, syy, szz, sxz, syz = st[3, p], st[1, p], st[2, p], st[4, p], st[5, p]
        ax = diff(st[0, p - 1], st[0, p], st[0, p + 1], st[0, p + 2])
        ax += along_y(sxy, 0.0, 0.0, 0.0, 0.0, False) + along_z(sxz, False)
        ay = diff(st[3, p - 2], st[3, p - 1], sxy, st[3, p + 1])
        ay += along_y(syy, 0.0, 0.0, 0.0, 0.0, True) + along_z(syz, False)
        az = diff(st[4, p - 2], st[4, p - 1], sxz, st[4, p + 1])
        az += along_y(syz, 0.0, 0.0, 0.0, 0.0, False) + along_z(szz, True)
        scale = time_step * buo[x]
        u[0, p] = vel[0, x] + scale * (ax + force[0, x])
        u[1, p] = vel[1, x] + scale * (ay + force[1, x])
        u[2, p] = vel[2, x] + scale * (az + force[2, x])

    planes(velocity_plane)
    for k in range(4):
        axis, upward = k // 2, k % 2 == 1
        for at, (name, index) in enumerate(speed_of_p if upward else speed_of_q):
            speed_out[k, at] = layer(u, axis, component[axis][name], index)
    start("speed")

    def add_force(tile, n, pieces):
        parts = spread(tile, n, [piece for _, piece in pieces])
        for (region, (axis, layers, first, count)), part in zip(pieces, parts):
            base = {0: 0, 1: 14, 2: -2, 3: 16}[region % 2 + 2 * (region // 4)]
            at = 0
            for i in range(3):
                for a in layers:
                    forces[region, i, a - base, first : first + count, :] += part[at : at + count]
                    at += count

    every = (0, 16)
    block = {-1: (0, 8), 0: every, 1: (8, 8)}
    add_force(me, (0, 0), [
        (4, (0, (-1,), *every)), (5, (0, (16, 17), *every)), (6, (1, (-1,), *every)), (7, (1, (16, 17), *every)),
    ])
    low_in, high_in, low_out, high_out = (0, 1), (15,), (-2, -1), (16, 17)
    for n in order:
        tx, ty = n
        if tx and ty:
            arrive("corner", n)
            tile = unpack(corner_in[corners.index(n), 0:8, :])
        else:
            arrive("face", n)
            tile = unpack(face_in[sides.index(n), 0:8, :])
        pieces = []
        if tx:
            pieces.append((0 if tx < 0 else 1, (0, low_in if tx < 0 else high_in, *block[ty])))
            for sy in ((-1, 1) if ty == 0 else (ty,)):
                layers = (low_out if sy < 0 else high_out) if ty else ((-1,) if sy < 0 else (16, 17))
                pieces.append((6 if sy < 0 else 7, (1, layers, *block[tx])))
        else:
            pieces.append((2 if ty < 0 else 3, (1, low_in if ty < 0 else high_in, *every)))
        if ty:
            for sx in ((-1, 1) if tx == 0 else (tx,)):
                layers = (low_out if sx < 0 else high_out) if tx else ((-1,) if sx < 0 else (16, 17))
                pieces.append((4 if sx < 0 else 5, (0, layers, *block[ty])))
        add_force(tile, n, pieces)

    row = lax.broadcasted_iota(jnp.int32, (16, 128), 0)
    for k in (3, 1, 0, 2):
        axis, upward = k // 2, k % 2 == 1
        names = component[axis]
        mine = lambda name, index: layer(st, axis, field[axis][name], index)
        layers = stress_of_q if upward else stress_of_p
        theirs = lambda name, index: face_in[k, pl.ds(head + 16 * layers.index((name, index)), 16), :]
        added = give(theirs, not upward)
        base = 14 if upward else 0
        for name in ("n", "t", "r"):
            c = names[name]
            for index in (base, base + 1):
                if upward and index == 14 and name != "n":
                    continue
                acc = forces[k, c, index - base]
                if (name, index) in added:
                    acc = acc + added[name, index]()
                if axis == 0:
                    u[c, 2 + index] += time_step * buo[index] * acc
                else:
                    u[c, 2:18, index, :] = u[c, 2:18, index, :] + time_step * buo[:, index, :] * acc
        arrive("speed", sides[k])
        added = give(mine, upward)
        other = 1 - axis
        for at, (name, index) in enumerate(speed_of_q if upward else speed_of_p):
            c = names[name]
            near = index if upward else index - 14
            acc = forces[4 + k, c, near] + added[name, index]()
            for along in (-1, 1):
                n = (sides[k][0] + (0 if axis == 0 else along), sides[k][1] + (along if axis == 0 else 0))
                cells = lists[n]

                def cell(what, where):
                    key = (field[other][what], index, where) if axis == 0 else (field[other][what], where, index)
                    r = 6 + cells.index(key)
                    return corner_in[corners.index(n), r : r + 1, :]

                for (what, where), value in give(cell, along < 0).items():
                    if what == role[other][c]:
                        acc = acc + jnp.where(row == where, value(), 0.0)
            b_at = head + 16 * (len(layers) + near)
            total = speed_in[k, at] + time_step * face_in[k, b_at : b_at + 16, :] * acc
            if axis == 0:
                u[c, (18 if upward else 0) + near] = total
            else:
                speed_in[k, at] = total

    loads["lam"].wait()
    loads["mu"].wait()

    def stress_plane(x):
        p = x + 2

        def low(k):
            return speed_in[2, k, pl.ds(x, 1), :]

        def high(k):
            return speed_in[3, k, pl.ds(x, 1), :]

        ux, uy, uz = u[0, p], u[1, p], u[2, p]
        nv[0, x], nv[1, x], nv[2, x] = ux, uy, uz
        exx = diff(u[0, p - 2], u[0, p - 1], ux, u[0, p + 1])
        eyy = along_y(uy, low(0), low(1), high(0), None, False)
        ezz = along_z(uz, False)
        two = (2.0 * time_step) * mu[x]
        press = time_step * lam[x] * (exx + eyy + ezz)
        shear = time_step * mu[x]
        ns[0, x] = st[0, p] + (press + two * exx)
        ns[1, x] = st[1, p] + (press + two * eyy)
        ns[2, x] = st[2, p] + (press + two * ezz)
        ns[3, x] = st[3, p] + shear * (
            along_y(ux, None, low(2), high(1), high(2), True)
            + diff(u[1, p - 1], uy, u[1, p + 1], u[1, p + 2])
        )
        ns[4, x] = st[4, p] + shear * (along_z(ux, True) + diff(u[2, p - 1], uz, u[2, p + 1], u[2, p + 2]))
        ns[5, x] = st[5, p] + shear * (along_z(uy, True) + along_y(uz, None, low(3), high(3), high(4), True))

    planes(stress_plane)
    for (what, back), copy in copies.items():
        @pl.when(there(-back[0], -back[1]))
        def _():
            copy.wait_send()


def store(v, s, v_out, s_out, sem):
    copies = [pltpu.make_async_copy(v, v_out, sem.at[0]), pltpu.make_async_copy(s, s_out, sem.at[1])]
    for copy in copies:
        copy.start()
    for copy in copies:
        copy.wait()


def local(velocity, stress, buoyancy, lame_lambda, shear_modulus, moment, signal, sx, sy, sz, count, *, nx, ny):
    hbm = pl.BlockSpec(memory_space=pltpu.HBM)
    on_chip = pl.BlockSpec(memory_space=pltpu.VMEM)
    vmem = pltpu.VMEM
    keep = functools.partial(pltpu.with_memory_space_constraint, memory_space=pltpu.VMEM)
    leave = functools.partial(pltpu.with_memory_space_constraint, memory_space=pltpu.HBM)
    args = (velocity, stress, buoyancy, lame_lambda, shear_modulus, jnp.transpose(moment, (0, 2, 1, 3)), signal, sx, sy, sz)
    done = pl.pallas_call(
        functools.partial(kernel, nx, ny),
        out_shape=(vmem(velocity.shape, F32), vmem(stress.shape, F32)),
        in_specs=[hbm] * 10 + [pl.BlockSpec(memory_space=pltpu.SMEM)],
        out_specs=(on_chip, on_chip),
        scratch_shapes=[
            vmem((3, 16, 16, 128), F32),
            vmem((6, 20, 16, 128), F32),
            vmem((16, 16, 128), F32),
            vmem((16, 16, 128), F32),
            vmem((16, 16, 128), F32),
            vmem((1, 6, 1, 64), F32),
            vmem((1, 1, 64), F32),
            vmem((1, 1, 64), jnp.int32),
            vmem((1, 1, 64), jnp.int32),
            vmem((1, 1, 64), jnp.int32),
            vmem((3, 16, 16, 128), F32),
            vmem((3, 20, 16, 128), F32),
            vmem((8, 3, 2, 16, 128), F32),
            vmem((4, 120, 128), F32),
            vmem((4, 120, 128), F32),
            vmem((4, 5, 16, 128), F32),
            vmem((4, 5, 16, 128), F32),
            vmem((4, 24, 128), F32),
            vmem((4, 24, 128), F32),
            pltpu.SemaphoreType.DMA((10,)),
            pltpu.SemaphoreType.DMA((12,)),
            pltpu.SemaphoreType.DMA((12,)),
        ],
        compiler_params=pltpu.CompilerParams(
            collective_id=0, has_side_effects=True, vmem_limit_bytes=48 * 1024 * 1024
        ),
        name="elastic_step",
    )(*map(leave, args), count)
    return pl.pallas_call(
        store,
        out_shape=(pltpu.HBM(velocity.shape, F32), pltpu.HBM(stress.shape, F32)),
        in_specs=[on_chip] * 2,
        out_specs=(hbm, hbm),
        scratch_shapes=[pltpu.SemaphoreType.DMA((2,))],
        name="store_fields",
    )(*map(keep, done))


def solution(mesh):
    field = P(None, "gx", "gy", None)
    cells = P("gx", "gy", None)
    in_specs = (field, field, cells, cells, cells, P("gx", "gy", None, None)) + (cells,) * 5
    step = functools.partial(local, nx=mesh.shape["gx"], ny=mesh.shape["gy"])
    return jax.shard_map(step, mesh=mesh, in_specs=in_specs, out_specs=(field, field), check_vma=False)
```

```python
import functools
import jax
import jax.numpy as jnp
from jax import lax
from jax.sharding import PartitionSpec as P
import jax.experimental.pallas as pl
import jax.experimental.pallas.tpu as pltpu

MESH = pl.DeviceIdType.MESH
F32 = jnp.float32
BF16 = jnp.bfloat16

c1 = 9.0 / 8.0
c2 = -1.0 / 24.0
time_step = 0.1
d_table = (1.0, -27.0, 27.0, -1.0)
w_table = (-1.0, 9.0, 9.0, -1.0)
unscale = 1.0 / (16.0 * 16.0 * 24.0)
pairs = ((0, 3, 4), (3, 1, 5), (4, 5, 2))
neighbours = ((-1, -1), (-1, 0), (-1, 1), (0, -1), (0, 1), (1, -1), (1, 0), (1, 1))


stress_of_p = (("n", 15), ("t", 14), ("t", 15), ("r", 14), ("r", 15))
stress_of_q = (("n", 0), ("n", 1), ("t", 0), ("r", 0))
speed_of_p = (("n", 14), ("n", 15), ("t", 15), ("r", 15))
speed_of_q = (("n", 0), ("t", 0), ("t", 1), ("r", 0), ("r", 1))
component = ({"n": 0, "t": 1, "r": 2}, {"n": 1, "t": 0, "r": 2})
field = ({"n": 0, "t": 3, "r": 4}, {"n": 1, "t": 3, "r": 5})
role = tuple({c: r for r, c in names.items()} for names in component)
head = 8
early = ((0, 1), (1, 1), (-1, 1), (1, 0), (-1, 0))
late = ((1, -1), (-1, -1), (0, -1))


def give(get, upward):
    if upward:
        return {
            ("n", 0): lambda: -c2 * get("n", 15),
            ("t", 0): lambda: -c1 * get("t", 15) - c2 * get("t", 14),
            ("t", 1): lambda: -c2 * get("t", 15),
            ("r", 0): lambda: -c1 * get("r", 15) - c2 * get("r", 14),
            ("r", 1): lambda: -c2 * get("r", 15),
        }
    return {
        ("n", 14): lambda: c2 * get("n", 0),
        ("n", 15): lambda: c1 * get("n", 0) + c2 * get("n", 1),
        ("t", 15): lambda: c2 * get("t", 0),
        ("r", 15): lambda: c2 * get("r", 0),
    }


def corner_cells(sx, sy):
    cells = []
    for axis, (across, along) in enumerate(((sx, sy), (sy, sx))):
        other = 1 - axis
        for name, at in speed_of_p if across < 0 else speed_of_q:
            part = role[other][component[axis][name]]
            for what, index in stress_of_p if along < 0 else stress_of_q:
                if what == part:
                    cell = (field[other][what], at, index) if axis == 0 else (field[other][what], index, at)
                    if cell not in cells:
                        cells.append(cell)
    return cells


def lookup(offset, table):
    value = jnp.where(offset == 3, table[3], 0.0)
    for k in (2, 1, 0):
        value = jnp.where(offset == k, table[k], value)
    return value


def halves(low, high):
    lane = lax.broadcasted_iota(jnp.int32, (1, 128), 1)
    return jnp.where(lane < 64, low, high)


def stencil(length, start, position, table):
    cell = lax.broadcasted_iota(jnp.int32, (length, 128), 0) + start
    return lookup(cell - position + 1, table)


def unpack(rows):
    p = [rows[i : i + 1, :] for i in range(3)]
    mixed = [rows[3 + i : 4 + i, :] for i in range(3)]
    q = [halves(row, 0.0) for row in mixed]
    at = [halves(pltpu.roll(row, 64, 1), row).astype(jnp.int32) for row in mixed]
    return p, q, at


def depth_weights(pz):
    table = [halves(w, d) for w, d in zip(w_table, d_table)]
    weights = stencil(128, 0, pz, table).astype(BF16)
    return jnp.concatenate([weights, weights], axis=1)


def spread(tile, shift, pieces):
    p, q, (px, py, pz) = tile
    mixed = [halves(d, w) for w, d in zip(w_table, d_table)]
    position = (px + 16 * shift[0], py + 16 * shift[1])
    tables = ((mixed, w_table), (w_table, d_table))
    rows = []
    for axis, layers, start, count in pieces:
        one = [stencil(len(layers), layers[0], position[axis], table) for table in tables[axis]]
        two = [stencil(count, start, position[1 - axis], table) for table in tables[1 - axis]]
        for i in range(3):
            first, second = p[i] * one[0], q[i] * one[1]
            for k in range(len(layers)):
                rows.append(first[k : k + 1, :] * two[0] + second[k : k + 1, :] * two[1])
    value = jnp.concatenate(rows, axis=0)
    high = value.astype(BF16)
    low = (value - high.astype(F32)).astype(BF16)
    result = lax.dot_general(
        jnp.concatenate([high, low], axis=1), depth_weights(pz), (((1,), (1,)), ((), ())),
        preferred_element_type=F32,
    )
    parts, at = [], 0
    for axis, layers, start, count in pieces:
        size = 3 * len(layers) * count
        parts.append(result[at : at + size])
        at += size
    return parts


def diff(m2, m1, f, p1):
    return c1 * (f - m1) + c2 * (p1 - m2)


def along_y(f, low2, low1, high1, high2, forward):
    iy = lax.broadcasted_iota(jnp.int32, f.shape, 0)
    m1 = jnp.where(iy == 0, low1, pltpu.roll(f, 1, 0))
    p1 = jnp.where(iy == 15, high1, pltpu.roll(f, 15, 0))
    if forward:
        p2 = jnp.where(iy == 15, high2, jnp.where(iy == 14, high1, pltpu.roll(f, 14, 0)))
        return diff(m1, f, p1, p2)
    m2 = jnp.where(iy == 0, low2, jnp.where(iy == 1, low1, pltpu.roll(f, 2, 0)))
    return diff(m2, m1, f, p1)


def along_z(f, forward):
    iz = lax.broadcasted_iota(jnp.int32, f.shape, 1)
    m1 = jnp.where(iz < 1, 0.0, pltpu.roll(f, 1, 1))
    p1 = jnp.where(iz > 126, 0.0, pltpu.roll(f, 127, 1))
    if forward:
        p2 = jnp.where(iz > 125, 0.0, pltpu.roll(f, 126, 1))
        return diff(m1, f, p1, p2)
    m2 = jnp.where(iz < 2, 0.0, pltpu.roll(f, 2, 1))
    return diff(m2, m1, f, p1)


def planes(plane):
    def group(i, _):
        for k in range(4):
            plane(i * 4 + k)
        return 0

    lax.fori_loop(0, 4, group, 0)


def kernel(
    nx, ny,
    v_in, s_in, b_in, l_in, m_in, mom_in, sig_in, px_in, py_in, pz_in, cnt_in,
    u, st, lam, mu, edge,
    vel, buo, mom, sig, px, py, pz,
    force, forces, face_out, face_in, speed_out, speed_in, corner_out, corner_in,
    load_sem, send_sem, recv_sem,
):
    gx, gy = lax.axis_index("gx"), lax.axis_index("gy")

    def there(dx, dy):
        ok = True
        for at, step, count in ((gx, dx, nx), (gy, dy, ny)):
            if step:
                ok = ok & (at > 0) if step < 0 else ok & (at < count - 1)
        return ok

    barrier = pltpu.get_barrier_semaphore()
    expected = 0
    for dx, dy in neighbours:
        expected = expected + there(dx, dy).astype(jnp.int32)

        @pl.when(there(dx, dy))
        def _():
            pl.semaphore_signal(barrier, inc=1, device_id=(gx + dx, gy + dy), device_id_type=MESH)

    loads = {}
    for k, (name, src, dst) in enumerate((
        ("mom", mom_in, mom), ("sig", sig_in, sig), ("px", px_in, px), ("py", py_in, py),
        ("pz", pz_in, pz),
        ("st", s_in, st.at[:, 2:18]), ("buo", b_in, buo), ("vel", v_in, vel),
        ("lam", l_in, lam), ("mu", m_in, mu),
    )):
        loads[name] = pltpu.make_async_copy(src, dst, load_sem.at[k])
        loads[name].start()

    sides = ((-1, 0), (1, 0), (0, -1), (0, 1))
    corners = ((-1, -1), (-1, 1), (1, -1), (1, 1))
    lists = {n: corner_cells(*n) for n in corners}

    for f in (0, 3, 4):
        st[f, 0:2] = jnp.zeros((2, 16, 128), F32)
        st[f, 18:20] = jnp.zeros((2, 16, 128), F32)
    forces[...] = jnp.zeros((12, 3, 2, 16, 128), F32)
    for k, n in enumerate(sides):
        @pl.when(jnp.logical_not(there(*n)))
        def _():
            face_in[k] = jnp.zeros((120, 128), F32)
            speed_in[k] = jnp.zeros((5, 16, 128), F32)

    for k, n in enumerate(corners):
        @pl.when(jnp.logical_not(there(*n)))
        def _():
            corner_in[k] = jnp.zeros((24, 128), F32)

    for name in ("mom", "sig", "px", "py", "pz"):
        loads[name].wait()
    lane = lax.broadcasted_iota(jnp.int32, (1, 64), 1)
    live = (lane < cnt_in[0, 0, 0]).astype(F32)
    scaled = sig[0] * live * (-unscale)
    amp = [mom[0, r] * scaled for r in range(6)]
    rows = [jnp.concatenate([amp[pairs[i][0]], amp[pairs[i][2]]], axis=1) for i in range(3)]
    for i, ref in enumerate((px, py, pz)):
        rows.append(jnp.concatenate([amp[pairs[i][1]], ref[0].astype(F32)], axis=1))
    own_rows = jnp.concatenate(rows, axis=0)
    for k in range(4):
        face_out[k, 0:6, :] = own_rows
        face_out[k, 6:8, :] = jnp.zeros((2, 128), F32)
        corner_out[k, 0:6, :] = own_rows

    def remote(k, src, dst, n):
        return pltpu.make_async_remote_copy(
            src_ref=src, dst_ref=dst, send_sem=send_sem.at[k], recv_sem=recv_sem.at[k],
            device_id=(gx + n[0], gy + n[1]), device_id_type=MESH,
        )

    copies = {}
    for k, n in enumerate(sides):
        upward = k % 2 == 1
        size = head + 16 * (len(stress_of_p if upward else stress_of_q) + 2)
        count = len(speed_of_p if upward else speed_of_q)
        back = (-n[0], -n[1])
        copies["face", back] = remote(k, face_out.at[k, 0:size], face_in.at[k ^ 1, 0:size], n)
        copies["speed", back] = remote(4 + k, speed_out.at[k, 0:count], speed_in.at[k ^ 1, 0:count], n)
    for k, n in enumerate(corners):
        back = (-n[0], -n[1])
        size = -(-(6 + len(lists[back])) // 8) * 8
        copies["corner", back] = remote(8 + k, corner_out.at[k, 0:size], corner_in.at[3 - k, 0:size], n)

    def start(kind):
        for (what, back), copy in copies.items():
            if what == kind:
                @pl.when(there(-back[0], -back[1]))
                def _():
                    copy.start()

    def arrive(kind, n):
        @pl.when(there(*n))
        def _():
            copies[kind, n].wait_recv()

    def layer(ref, axis, f, at):
        return ref[f, at + 2] if axis == 0 else ref[f, 2:18, at, :]

    loads["st"].wait()
    loads["buo"].wait()
    for k in range(4):
        axis, upward = k // 2, k % 2 == 1
        at = head
        for name, index in stress_of_p if upward else stress_of_q:
            face_out[k, at : at + 16, :] = layer(st, axis, field[axis][name], index)
            at += 16
        for index in (14, 15) if upward else (0, 1):
            face_out[k, at : at + 16, :] = buo[index] if axis == 0 else buo[:, index, :]
            at += 16
    for k, n in enumerate(corners):
        for r, (f, x, y) in enumerate(lists[-n[0], -n[1]]):
            corner_out[k, 6 + r : 7 + r, :] = st[f, 2 + x, y : y + 1, :]
        if 6 + len(lists[-n[0], -n[1]]) > 16:
            corner_out[k, 6 + len(lists[-n[0], -n[1]]) : 24, :] = jnp.zeros((18 - len(lists[-n[0], -n[1]]), 128), F32)

    pl.semaphore_wait(barrier, expected)
    start("face")
    start("corner")

    me = unpack(own_rows)
    force[...] = spread(me, (0, 0), [(0, tuple(range(16)), 0, 16)])[0].reshape(3, 16, 16, 128)
    loads["vel"].wait()

    def velocity_plane(x):
        p = x + 2
        sxy, syy, szz, sxz, syz = st[3, p], st[1, p], st[2, p], st[4, p], st[5, p]
        ax = diff(st[0, p - 1], st[0, p], st[0, p + 1], st[0, p + 2])
        ax += along_y(sxy, 0.0, 0.0, 0.0, 0.0, False) + along_z(sxz, False)
        ay = diff(st[3, p - 2], st[3, p - 1], sxy, st[3, p + 1])
        ay += along_y(syy, 0.0, 0.0, 0.0, 0.0, True) + along_z(syz, False)
        az = diff(st[4, p - 2], st[4, p - 1], sxz, st[4, p + 1])
        az += along_y(syz, 0.0, 0.0, 0.0, 0.0, False) + along_z(szz, True)
        scale = time_step * buo[x]
        u[0, p] = vel[0, x] + scale * (ax + force[0, x])
        u[1, p] = vel[1, x] + scale * (ay + force[1, x])
        u[2, p] = vel[2, x] + scale * (az + force[2, x])

    planes(velocity_plane)
    for k in range(4):
        axis, upward = k // 2, k % 2 == 1
        for at, (name, index) in enumerate(speed_of_p if upward else speed_of_q):
            speed_out[k, at] = layer(u, axis, component[axis][name], index)
    start("speed")

    def add_force(tile, n, pieces, shelf=None):
        parts = spread(tile, n, [piece for _, piece in pieces])
        for (region, (axis, layers, first, count)), part in zip(pieces, parts):
            base = {0: 0, 1: 14, 2: -2, 3: 16}[region % 2 + 2 * (region // 4)]
            region = (shelf or {}).get(region, region)
            at = 0
            for i in range(3):
                for a in layers:
                    forces[region, i, a - base, first : first + count, :] += part[at : at + count]
                    at += count

    every = (0, 16)
    block = {-1: (0, 8), 0: every, 1: (8, 8)}
    add_force(me, (0, 0), [
        (4, (0, (-1,), *every)), (5, (0, (16, 17), *every)), (6, (1, (-1,), *every)), (7, (1, (16, 17), *every)),
    ])
    low_in, high_in, low_out, high_out = (0, 1), (15,), (-2, -1), (16, 17)
    shelf = {0: 8, 1: 9, 4: 10, 5: 11}

    def tile_force(n):
        tx, ty = n
        if tx and ty:
            tile = unpack(corner_in[corners.index(n), 0:8, :])
        else:
            tile = unpack(face_in[sides.index(n), 0:8, :])
        pieces = []
        if tx:
            pieces.append((0 if tx < 0 else 1, (0, low_in if tx < 0 else high_in, *block[ty])))
            for sy in ((-1, 1) if ty == 0 else (ty,)):
                layers = (low_out if sy < 0 else high_out) if ty else ((-1,) if sy < 0 else (16, 17))
                pieces.append((6 if sy < 0 else 7, (1, layers, *block[tx])))
        else:
            pieces.append((2 if ty < 0 else 3, (1, low_in if ty < 0 else high_in, *every)))
        if ty:
            for sx in ((-1, 1) if tx == 0 else (tx,)):
                layers = (low_out if sx < 0 else high_out) if tx else ((-1,) if sx < 0 else (16, 17))
                pieces.append((4 if sx < 0 else 5, (0, layers, *block[ty])))
        add_force(tile, n, pieces, shelf if n in late else None)

    def come(tiles):
        for n in tiles:
            arrive("corner" if n[0] and n[1] else "face", n)
        for n in tiles:
            tile_force(n)

    def corner_share(k, name, index, along):
        axis = k // 2
        other = 1 - axis
        n = (sides[k][0] + (0 if axis == 0 else along), sides[k][1] + (along if axis == 0 else 0))

        def cell(what, where):
            key = (field[other][what], index, where) if axis == 0 else (field[other][what], where, index)
            r = 6 + lists[n].index(key)
            return corner_in[corners.index(n), r : r + 1, :]

        return [
            (where, value())
            for (what, where), value in give(cell, along < 0).items()
            if what == role[other][component[axis][name]]
        ]

    row = lax.broadcasted_iota(jnp.int32, (16, 128), 0)

    def share(k):
        axis, upward = k // 2, k % 2 == 1
        names = component[axis]
        layers = stress_of_q if upward else stress_of_p

        def mine(name, index):
            return layer(st, axis, field[axis][name], index)

        def theirs(name, index):
            at = head + 16 * layers.index((name, index))
            return face_in[k, at : at + 16, :]

        added = give(theirs, not upward)
        base = 14 if upward else 0
        for name in ("n", "t", "r"):
            c = names[name]
            for index in (base, base + 1):
                if upward and index == 14 and name != "n":
                    continue
                acc = forces[k, c, index - base]
                if (name, index) in added:
                    acc = acc + added[name, index]()
                if axis == 0:
                    u[c, 2 + index] += time_step * buo[index] * acc
                else:
                    u[c, 2:18, index, :] = u[c, 2:18, index, :] + time_step * buo[:, index, :] * acc
        arrive("speed", sides[k])
        added = give(mine, upward)
        for at, (name, index) in enumerate(speed_of_q if upward else speed_of_p):
            c = names[name]
            near = index if upward else index - 14
            acc = forces[4 + k, c, near] + added[name, index]()
            for along in (1,) if axis == 0 else (-1, 1):
                for where, value in corner_share(k, name, index, along):
                    acc = acc + jnp.where(row == where, value, 0.0)
            b_at = head + 16 * (len(layers) + near)
            total = speed_in[k, at] + time_step * face_in[k, b_at : b_at + 16, :] * acc
            if axis == 0:
                u[c, (18 if upward else 0) + near] = total
            else:
                edge[k - 2, at] = total

    def late_share(k):
        upward = k == 1
        for index in (15,) if upward else (0, 1):
            for c in range(3):
                acc = forces[shelf[k], c, index - (14 if upward else 0), 0:8, :]
                u[c, 2 + index, 0:8, :] += time_step * buo[index, 0:8, :] * acc
        for name, index in speed_of_q if upward else speed_of_p:
            c = component[0][name]
            near = index if upward else index - 14
            acc = forces[shelf[4 + k], c, near, 0:8, :]
            for where, value in corner_share(k, name, index, -1):
                acc = acc + jnp.where(row[0:8] == where, value, 0.0)
            b_at = head + 16 * (len(stress_of_q if upward else stress_of_p) + near)
            u[c, (18 if upward else 0) + near, 0:8, :] += time_step * face_in[k, b_at : b_at + 8, :] * acc

    come(early)
    for k in (3, 1, 0):
        share(k)
    come(late)
    for k in (1, 0):
        late_share(k)
    share(2)

    loads["lam"].wait()
    loads["mu"].wait()

    for (what, back), copy in copies.items():
        @pl.when(there(-back[0], -back[1]))
        def _():
            copy.wait_send()


def finish(u, st, lam, mu, edge, v_out, s_out, ns, sem):
    copies = [pltpu.make_async_copy(u.at[:, 2:18], v_out, sem.at[4])]
    copies[0].start()

    def stress_plane(x):
        p = x + 2

        def low(k):
            return edge[0, k, x : x + 1, :]

        def high(k):
            return edge[1, k, x : x + 1, :]

        ux, uy, uz = u[0, p], u[1, p], u[2, p]
        exx = diff(u[0, p - 2], u[0, p - 1], ux, u[0, p + 1])
        eyy = along_y(uy, low(0), low(1), high(0), None, False)
        ezz = along_z(uz, False)
        two = (2.0 * time_step) * mu[x]
        press = time_step * lam[x] * (exx + eyy + ezz)
        shear = time_step * mu[x]
        ns[0, x] = st[0, p] + (press + two * exx)
        ns[1, x] = st[1, p] + (press + two * eyy)
        ns[2, x] = st[2, p] + (press + two * ezz)
        ns[3, x] = st[3, p] + shear * (
            along_y(ux, None, low(2), high(1), high(2), True)
            + diff(u[1, p - 1], uy, u[1, p + 1], u[1, p + 2])
        )
        ns[4, x] = st[4, p] + shear * (along_z(ux, True) + diff(u[2, p - 1], uz, u[2, p + 1], u[2, p + 2]))
        ns[5, x] = st[5, p] + shear * (along_z(uy, True) + along_y(uz, None, low(3), high(3), high(4), True))

    for part in range(4):
        cells = pl.ds(4 * part, 4)
        for x in range(4 * part, 4 * part + 4):
            stress_plane(x)
        copies.append(pltpu.make_async_copy(ns.at[:, cells], s_out.at[:, cells], sem.at[part]))
        copies[-1].start()
    for copy in copies:
        copy.wait()


def kept(*shape):
    return pltpu.VMEM(shape, F32)


def result(shape):
    return pltpu.HBM(shape, F32)


def local(velocity, stress, buoyancy, lame_lambda, shear_modulus, moment, signal, sx, sy, sz, count, *, nx, ny):
    hbm = pl.BlockSpec(memory_space=pltpu.HBM)
    on_chip = pl.BlockSpec(memory_space=pltpu.VMEM)
    vmem = pltpu.VMEM
    keep = functools.partial(pltpu.with_memory_space_constraint, memory_space=pltpu.VMEM)
    leave = functools.partial(pltpu.with_memory_space_constraint, memory_space=pltpu.HBM)
    args = (velocity, stress, buoyancy, lame_lambda, shear_modulus, jnp.transpose(moment, (0, 2, 1, 3)), signal, sx, sy, sz)
    done = pl.pallas_call(
        functools.partial(kernel, nx, ny),
        out_shape=(kept(3, 20, 16, 128), kept(6, 20, 16, 128), kept(16, 16, 128), kept(16, 16, 128), kept(2, 5, 16, 128)),
        in_specs=[hbm] * 10 + [pl.BlockSpec(memory_space=pltpu.SMEM)],
        out_specs=(on_chip,) * 5,
        scratch_shapes=[
            vmem((3, 16, 16, 128), F32),
            vmem((16, 16, 128), F32),
            vmem((1, 6, 1, 64), F32),
            vmem((1, 1, 64), F32),
            vmem((1, 1, 64), jnp.int32),
            vmem((1, 1, 64), jnp.int32),
            vmem((1, 1, 64), jnp.int32),
            vmem((3, 16, 16, 128), F32),
            vmem((12, 3, 2, 16, 128), F32),
            vmem((4, 120, 128), F32),
            vmem((4, 120, 128), F32),
            vmem((4, 5, 16, 128), F32),
            vmem((4, 5, 16, 128), F32),
            vmem((4, 24, 128), F32),
            vmem((4, 24, 128), F32),
            pltpu.SemaphoreType.DMA((10,)),
            pltpu.SemaphoreType.DMA((12,)),
            pltpu.SemaphoreType.DMA((12,)),
        ],
        compiler_params=pltpu.CompilerParams(
            collective_id=0, has_side_effects=True, vmem_limit_bytes=48 * 1024 * 1024
        ),
        name="elastic_step",
    )(*map(leave, args), count)
    return pl.pallas_call(
        finish,
        out_shape=(result(velocity.shape), result(stress.shape)),
        in_specs=[on_chip] * 5,
        out_specs=(hbm, hbm),
        scratch_shapes=[vmem(stress.shape, F32), pltpu.SemaphoreType.DMA((5,))],
        name="new_stress",
    )(*map(keep, done))


def solution(mesh):
    field = P(None, "gx", "gy", None)
    cells = P("gx", "gy", None)
    in_specs = (field, field, cells, cells, cells, P("gx", "gy", None, None)) + (cells,) * 5
    step = functools.partial(local, nx=mesh.shape["gx"], ny=mesh.shape["gy"])
    return jax.shard_map(step, mesh=mesh, in_specs=in_specs, out_specs=(field, field), check_vma=False)
```

```python
import functools
import jax
import jax.numpy as jnp
from jax import lax
from jax.sharding import PartitionSpec as P
import jax.experimental.pallas as pl
import jax.experimental.pallas.tpu as pltpu

MESH = pl.DeviceIdType.MESH
F32 = jnp.float32
BF16 = jnp.bfloat16

c1 = 9.0 / 8.0
c2 = -1.0 / 24.0
time_step = 0.1
d_table = (1.0, -27.0, 27.0, -1.0)
w_table = (-1.0, 9.0, 9.0, -1.0)
unscale = 1.0 / (16.0 * 16.0 * 24.0)
pairs = ((0, 3, 4), (3, 1, 5), (4, 5, 2))
neighbours = ((-1, -1), (-1, 0), (-1, 1), (0, -1), (0, 1), (1, -1), (1, 0), (1, 1))


stress_of_p = (("n", 15), ("t", 14), ("t", 15), ("r", 14), ("r", 15))
stress_of_q = (("n", 0), ("n", 1), ("t", 0), ("r", 0))
speed_of_p = (("n", 14), ("n", 15), ("t", 15), ("r", 15))
speed_of_q = (("n", 0), ("t", 0), ("t", 1), ("r", 0), ("r", 1))
component = ({"n": 0, "t": 1, "r": 2}, {"n": 1, "t": 0, "r": 2})
field = ({"n": 0, "t": 3, "r": 4}, {"n": 1, "t": 3, "r": 5})
role = tuple({c: r for r, c in names.items()} for names in component)
head = 8
early = ((0, 1), (1, 1), (-1, 1), (1, 0), (-1, 0))
late = ((1, -1), (-1, -1), (0, -1))


def give(get, upward):
    if upward:
        return {
            ("n", 0): lambda: -c2 * get("n", 15),
            ("t", 0): lambda: -c1 * get("t", 15) - c2 * get("t", 14),
            ("t", 1): lambda: -c2 * get("t", 15),
            ("r", 0): lambda: -c1 * get("r", 15) - c2 * get("r", 14),
            ("r", 1): lambda: -c2 * get("r", 15),
        }
    return {
        ("n", 14): lambda: c2 * get("n", 0),
        ("n", 15): lambda: c1 * get("n", 0) + c2 * get("n", 1),
        ("t", 15): lambda: c2 * get("t", 0),
        ("r", 15): lambda: c2 * get("r", 0),
    }


def corner_cells(sx, sy):
    cells = []
    for axis, (across, along) in enumerate(((sx, sy), (sy, sx))):
        other = 1 - axis
        for name, at in speed_of_p if across < 0 else speed_of_q:
            part = role[other][component[axis][name]]
            for what, index in stress_of_p if along < 0 else stress_of_q:
                if what == part:
                    cell = (field[other][what], at, index) if axis == 0 else (field[other][what], index, at)
                    if cell not in cells:
                        cells.append(cell)
    return cells


def lookup(offset, table):
    value = jnp.where(offset == 3, table[3], 0.0)
    for k in (2, 1, 0):
        value = jnp.where(offset == k, table[k], value)
    return value


def halves(low, high):
    lane = lax.broadcasted_iota(jnp.int32, (1, 128), 1)
    return jnp.where(lane < 64, low, high)


def stencil(length, start, position, table):
    cell = lax.broadcasted_iota(jnp.int32, (length, 128), 0) + start
    return lookup(cell - position + 1, table)


def unpack(rows):
    p = [rows[i : i + 1, :] for i in range(3)]
    mixed = [rows[3 + i : 4 + i, :] for i in range(3)]
    q = [halves(row, 0.0) for row in mixed]
    at = [halves(pltpu.roll(row, 64, 1), row).astype(jnp.int32) for row in mixed]
    return p, q, at


def depth_weights(pz):
    table = [halves(w, d) for w, d in zip(w_table, d_table)]
    weights = stencil(128, 0, pz, table).astype(BF16)
    return jnp.concatenate([weights, weights], axis=1)


def spread(tile, shift, pieces):
    p, q, (px, py, pz) = tile
    mixed = [halves(d, w) for w, d in zip(w_table, d_table)]
    position = (px + 16 * shift[0], py + 16 * shift[1])
    tables = ((mixed, w_table), (w_table, d_table))
    rows = []
    for axis, layers, start, count in pieces:
        one = [stencil(len(layers), layers[0], position[axis], table) for table in tables[axis]]
        two = [stencil(count, start, position[1 - axis], table) for table in tables[1 - axis]]
        for i in range(3):
            first, second = p[i] * one[0], q[i] * one[1]
            for k in range(len(layers)):
                rows.append(first[k : k + 1, :] * two[0] + second[k : k + 1, :] * two[1])
    value = jnp.concatenate(rows, axis=0)
    high = value.astype(BF16)
    low = (value - high.astype(F32)).astype(BF16)
    result = lax.dot_general(
        jnp.concatenate([high, low], axis=1), depth_weights(pz), (((1,), (1,)), ((), ())),
        preferred_element_type=F32,
    )
    parts, at = [], 0
    for axis, layers, start, count in pieces:
        size = 3 * len(layers) * count
        parts.append(result[at : at + size])
        at += size
    return parts


def diff(m2, m1, f, p1):
    return c1 * (f - m1) + c2 * (p1 - m2)


def along_y(f, low2, low1, high1, high2, forward):
    iy = lax.broadcasted_iota(jnp.int32, f.shape, 0)
    m1 = jnp.where(iy == 0, low1, pltpu.roll(f, 1, 0))
    p1 = jnp.where(iy == 15, high1, pltpu.roll(f, 15, 0))
    if forward:
        p2 = jnp.where(iy == 15, high2, jnp.where(iy == 14, high1, pltpu.roll(f, 14, 0)))
        return diff(m1, f, p1, p2)
    m2 = jnp.where(iy == 0, low2, jnp.where(iy == 1, low1, pltpu.roll(f, 2, 0)))
    return diff(m2, m1, f, p1)


def along_z(f, forward):
    iz = lax.broadcasted_iota(jnp.int32, f.shape, 1)
    m1 = jnp.where(iz < 1, 0.0, pltpu.roll(f, 1, 1))
    p1 = jnp.where(iz > 126, 0.0, pltpu.roll(f, 127, 1))
    if forward:
        p2 = jnp.where(iz > 125, 0.0, pltpu.roll(f, 126, 1))
        return diff(m1, f, p1, p2)
    m2 = jnp.where(iz < 2, 0.0, pltpu.roll(f, 2, 1))
    return diff(m2, m1, f, p1)


def stress_plane(u, st, lam, mu, edge, ns, x, rows):
    p = x + 2
    cells = pl.ds(rows, 8)

    def low(k):
        return edge[0, k, pl.ds(x, 1), :]

    def high(k):
        return edge[1, k, pl.ds(x, 1), :]

    def part(value):
        return value[rows : rows + 8]

    ux, uy, uz = u[0, p], u[1, p], u[2, p]
    exx = diff(u[0, p - 2, cells], u[0, p - 1, cells], part(ux), u[0, p + 1, cells])
    eyy = part(along_y(uy, low(0), low(1), high(0), None, False))
    ezz = along_z(part(uz), False)
    m = mu[x, cells]
    two = (2.0 * time_step) * m
    press = time_step * lam[x, cells] * (exx + eyy + ezz)
    shear = time_step * m
    ns[0, x, cells] = st[0, p, cells] + (press + two * exx)
    ns[1, x, cells] = st[1, p, cells] + (press + two * eyy)
    ns[2, x, cells] = st[2, p, cells] + (press + two * ezz)
    ns[3, x, cells] = st[3, p, cells] + shear * (
        part(along_y(ux, None, low(2), high(1), high(2), True))
        + diff(u[1, p - 1, cells], part(uy), u[1, p + 1, cells], u[1, p + 2, cells])
    )
    ns[4, x, cells] = st[4, p, cells] + shear * (
        along_z(part(ux), True) + diff(u[2, p - 1, cells], part(uz), u[2, p + 1, cells], u[2, p + 2, cells])
    )
    ns[5, x, cells] = st[5, p, cells] + shear * (
        along_z(part(uy), True) + part(along_y(uz, None, low(3), high(3), high(4), True))
    )


def planes(plane):
    def group(i, _):
        for k in range(4):
            plane(i * 4 + k)
        return 0

    lax.fori_loop(0, 4, group, 0)


def kernel(
    nx, ny,
    v_in, s_in, b_in, l_in, m_in, mom_in, sig_in, px_in, py_in, pz_in, cnt_in,
    u, st, lam, mu, edge, ns,
    vel, buo, mom, sig, px, py, pz,
    force, forces, face_out, face_in, speed_out, speed_in, corner_out, corner_in,
    load_sem, send_sem, recv_sem, ready,
):
    gx, gy = lax.axis_index("gx"), lax.axis_index("gy")

    def there(dx, dy):
        ok = True
        for at, step, count in ((gx, dx, nx), (gy, dy, ny)):
            if step:
                ok = ok & (at > 0) if step < 0 else ok & (at < count - 1)
        return ok

    barrier = pltpu.get_barrier_semaphore()
    expected, expected_below = 0, 0
    for dx, dy in neighbours:
        if dy >= 0:
            expected = expected + there(dx, dy).astype(jnp.int32)
        else:
            expected_below = expected_below + there(dx, dy).astype(jnp.int32)
        if dy <= 0:
            @pl.when(there(dx, dy))
            def _():
                pl.semaphore_signal(barrier, inc=1, device_id=(gx + dx, gy + dy), device_id_type=MESH)

    loads = {}
    for k, (name, src, dst) in enumerate((
        ("sxy", s_in.at[3, :, 8:16], st.at[3, 2:18, 8:16]), ("syy", s_in.at[1, :, 8:16], st.at[1, 2:18, 8:16]),
        ("syz", s_in.at[5, :, 8:16], st.at[5, 2:18, 8:16]), ("buo", b_in, buo),
        ("mom", mom_in, mom), ("sig", sig_in, sig), ("px", px_in, px), ("py", py_in, py),
        ("pz", pz_in, pz), ("sxx", s_in.at[0], st.at[0, 2:18]), ("sxz", s_in.at[4], st.at[4, 2:18]),
        ("sxy low", s_in.at[3, :, 0:8], st.at[3, 2:18, 0:8]), ("syy low", s_in.at[1, :, 0:8], st.at[1, 2:18, 0:8]),
        ("syz low", s_in.at[5, :, 0:8], st.at[5, 2:18, 0:8]), ("szz", s_in.at[2], st.at[2, 2:18]), ("vel", v_in, vel),
        ("lam", l_in, lam), ("mu", m_in, mu),
    )):
        loads[name] = pltpu.make_async_copy(src, dst, load_sem.at[k])
        loads[name].start()

    sides = ((-1, 0), (1, 0), (0, -1), (0, 1))
    corners = ((-1, -1), (-1, 1), (1, -1), (1, 1))
    lists = {n: corner_cells(*n) for n in corners}

    for f in (0, 3, 4):
        st[f, 0:2] = jnp.zeros((2, 16, 128), F32)
        st[f, 18:20] = jnp.zeros((2, 16, 128), F32)
    forces[...] = jnp.zeros((12, 3, 2, 16, 128), F32)
    for k, n in enumerate(sides):
        @pl.when(jnp.logical_not(there(*n)))
        def _():
            face_in[k] = jnp.zeros((120, 128), F32)
            speed_in[k] = jnp.zeros((5, 16, 128), F32)

    for k, n in enumerate(corners):
        @pl.when(jnp.logical_not(there(*n)))
        def _():
            corner_in[k] = jnp.zeros((24, 128), F32)

    pl.semaphore_wait(barrier, expected)
    for dx, dy in neighbours:
        if dy > 0:
            @pl.when(there(dx, dy))
            def _():
                pl.semaphore_signal(ready, inc=1, device_id=(gx + dx, gy + dy), device_id_type=MESH)

    for name in ("mom", "sig", "px", "py", "pz"):
        loads[name].wait()
    lane = lax.broadcasted_iota(jnp.int32, (1, 64), 1)
    live = (lane < cnt_in[0, 0, 0]).astype(F32)
    scaled = sig[0] * live * (-unscale)
    amp = [mom[0, r] * scaled for r in range(6)]
    rows = [jnp.concatenate([amp[pairs[i][0]], amp[pairs[i][2]]], axis=1) for i in range(3)]
    for i, ref in enumerate((px, py, pz)):
        rows.append(jnp.concatenate([amp[pairs[i][1]], ref[0].astype(F32)], axis=1))
    own_rows = jnp.concatenate(rows, axis=0)
    for k in range(4):
        face_out[k, 0:6, :] = own_rows
        face_out[k, 6:8, :] = jnp.zeros((2, 128), F32)
        corner_out[k, 0:6, :] = own_rows

    def remote(k, src, dst, n):
        return pltpu.make_async_remote_copy(
            src_ref=src, dst_ref=dst, send_sem=send_sem.at[k], recv_sem=recv_sem.at[k],
            device_id=(gx + n[0], gy + n[1]), device_id_type=MESH,
        )

    copies = {}
    for k, n in enumerate(sides):
        upward = k % 2 == 1
        size = head + 16 * (len(stress_of_p if upward else stress_of_q) + 2)
        count = len(speed_of_p if upward else speed_of_q)
        back = (-n[0], -n[1])
        copies["face", back] = remote(k, face_out.at[k, 0:size], face_in.at[k ^ 1, 0:size], n)
        copies["speed", back] = remote(4 + k, speed_out.at[k, 0:count], speed_in.at[k ^ 1, 0:count], n)
    for k, n in enumerate(corners):
        back = (-n[0], -n[1])
        size = -(-(6 + len(lists[back])) // 8) * 8
        copies["corner", back] = remote(8 + k, corner_out.at[k, 0:size], corner_in.at[3 - k, 0:size], n)

    def start(kind, towards):
        for k in towards:
            n = (corners if kind == "corner" else sides)[k]

            @pl.when(there(*n))
            def _():
                copies[kind, (-n[0], -n[1])].start()

    def arrive(kind, n):
        @pl.when(there(*n))
        def _():
            copies[kind, n].wait_recv()

    def layer(ref, axis, f, at):
        return ref[f, at + 2] if axis == 0 else ref[f, 2:18, at, :]

    def side_message(k):
        axis, upward = k // 2, k % 2 == 1
        at = head
        for name, index in stress_of_p if upward else stress_of_q:
            face_out[k, at : at + 16, :] = layer(st, axis, field[axis][name], index)
            at += 16
        for index in (14, 15) if upward else (0, 1):
            face_out[k, at : at + 16, :] = buo[index] if axis == 0 else buo[:, index, :]
            at += 16

    def corner_message(k):
        cells = lists[-corners[k][0], -corners[k][1]]
        for r, (f, x, y) in enumerate(cells):
            corner_out[k, 6 + r : 7 + r, :] = st[f, 2 + x, y : y + 1, :]
        if 6 + len(cells) > 16:
            corner_out[k, 6 + len(cells) : 24, :] = jnp.zeros((18 - len(cells), 128), F32)

    for name in ("sxy", "syy", "syz", "buo"):
        loads[name].wait()
    side_message(3)
    for name in ("sxx", "sxz"):
        loads[name].wait()
    corner_message(1)
    corner_message(3)
    start("corner", (1, 3))
    start("face", (3,))
    for name in ("sxy low", "syy low", "syz low"):
        loads[name].wait()
    side_message(1)
    side_message(0)
    start("face", (1, 0))
    side_message(2)
    corner_message(0)
    corner_message(2)

    me = unpack(own_rows)
    force[...] = spread(me, (0, 0), [(0, tuple(range(16)), 0, 16)])[0].reshape(3, 16, 16, 128)

    loads["szz"].wait()
    loads["vel"].wait()

    def velocity_plane(x, rows):
        p = x + 2
        cells = pl.ds(rows, 8)

        def part(value):
            return value[rows : rows + 8]

        def share_y(f, at, forward):
            return part(along_y(st[f, at], 0.0, 0.0, 0.0, 0.0, forward))

        def share_z(f, at, forward):
            return along_z(st[f, at, cells], forward)

        ax = diff(st[0, p - 1, cells], st[0, p, cells], st[0, p + 1, cells], st[0, p + 2, cells])
        ax += share_y(3, p, False) + share_z(4, p, False)
        ay = diff(st[3, p - 2, cells], st[3, p - 1, cells], st[3, p, cells], st[3, p + 1, cells])
        ay += share_y(1, p, True) + share_z(5, p, False)
        az = diff(st[4, p - 2, cells], st[4, p - 1, cells], st[4, p, cells], st[4, p + 1, cells])
        az += share_y(5, p, False) + share_z(2, p, True)
        scale = time_step * buo[x, cells]
        u[0, p, cells] = vel[0, x, cells] + scale * (ax + force[0, x, cells])
        u[1, p, cells] = vel[1, x, cells] + scale * (ay + force[1, x, cells])
        u[2, p, cells] = vel[2, x, cells] + scale * (az + force[2, x, cells])

    def speed_message(k):
        axis, upward = k // 2, k % 2 == 1
        for at, (name, index) in enumerate(speed_of_p if upward else speed_of_q):
            speed_out[k, at] = layer(u, axis, component[axis][name], index)

    planes(lambda x: velocity_plane(x, 8))
    speed_message(3)
    start("speed", (3,))
    planes(lambda x: velocity_plane(x, 0))
    for k in (1, 0, 2):
        speed_message(k)
    start("speed", (1, 0))

    def downward():
        @pl.when(gy > 0)
        def _():
            pl.semaphore_wait(ready, expected_below)

        start("face", (2,))
        start("corner", (0, 2))
        start("speed", (2,))

    patient = gy == ny // 2

    @pl.when(jnp.logical_not(patient))
    def _():
        downward()

    def add_force(tile, n, pieces, shelf=None):
        parts = spread(tile, n, [piece for _, piece in pieces])
        for (region, (axis, layers, first, count)), part in zip(pieces, parts):
            base = {0: 0, 1: 14, 2: -2, 3: 16}[region % 2 + 2 * (region // 4)]
            region = (shelf or {}).get(region, region)
            at = 0
            for i in range(3):
                for a in layers:
                    forces[region, i, a - base, first : first + count, :] += part[at : at + count]
                    at += count

    every = (0, 16)
    block = {-1: (0, 8), 0: every, 1: (8, 8)}
    add_force(me, (0, 0), [
        (4, (0, (-1,), *every)), (5, (0, (16, 17), *every)), (6, (1, (-1,), *every)), (7, (1, (16, 17), *every)),
    ])
    low_in, high_in, low_out, high_out = (0, 1), (15,), (-2, -1), (16, 17)
    shelf = {0: 8, 1: 9, 4: 10, 5: 11}

    def tile_force(n):
        tx, ty = n
        if tx and ty:
            tile = unpack(corner_in[corners.index(n), 0:8, :])
        else:
            tile = unpack(face_in[sides.index(n), 0:8, :])
        pieces = []
        if tx:
            pieces.append((0 if tx < 0 else 1, (0, low_in if tx < 0 else high_in, *block[ty])))
            for sy in ((-1, 1) if ty == 0 else (ty,)):
                layers = (low_out if sy < 0 else high_out) if ty else ((-1,) if sy < 0 else (16, 17))
                pieces.append((6 if sy < 0 else 7, (1, layers, *block[tx])))
        else:
            pieces.append((2 if ty < 0 else 3, (1, low_in if ty < 0 else high_in, *every)))
        if ty:
            for sx in ((-1, 1) if tx == 0 else (tx,)):
                layers = (low_out if sx < 0 else high_out) if tx else ((-1,) if sx < 0 else (16, 17))
                pieces.append((4 if sx < 0 else 5, (0, layers, *block[ty])))
        add_force(tile, n, pieces, shelf if n in late else None)

    def come(tiles):
        for n in tiles:
            arrive("corner" if n[0] and n[1] else "face", n)
        for n in tiles:
            tile_force(n)

    def corner_share(k, name, index, along):
        axis = k // 2
        other = 1 - axis
        n = (sides[k][0] + (0 if axis == 0 else along), sides[k][1] + (along if axis == 0 else 0))

        def cell(what, where):
            key = (field[other][what], index, where) if axis == 0 else (field[other][what], where, index)
            r = 6 + lists[n].index(key)
            return corner_in[corners.index(n), r : r + 1, :]

        return [
            (where, value())
            for (what, where), value in give(cell, along < 0).items()
            if what == role[other][component[axis][name]]
        ]

    row = lax.broadcasted_iota(jnp.int32, (16, 128), 0)

    def share(k):
        axis, upward = k // 2, k % 2 == 1
        names = component[axis]
        layers = stress_of_q if upward else stress_of_p

        def mine(name, index):
            return layer(st, axis, field[axis][name], index)

        def theirs(name, index):
            at = head + 16 * layers.index((name, index))
            return face_in[k, at : at + 16, :]

        added = give(theirs, not upward)
        base = 14 if upward else 0
        for name in ("n", "t", "r"):
            c = names[name]
            for index in (base, base + 1):
                if upward and index == 14 and name != "n":
                    continue
                acc = forces[k, c, index - base]
                if (name, index) in added:
                    acc = acc + added[name, index]()
                if axis == 0:
                    u[c, 2 + index] += time_step * buo[index] * acc
                else:
                    u[c, 2:18, index, :] = u[c, 2:18, index, :] + time_step * buo[:, index, :] * acc
        arrive("speed", sides[k])
        added = give(mine, upward)
        for at, (name, index) in enumerate(speed_of_q if upward else speed_of_p):
            c = names[name]
            near = index if upward else index - 14
            acc = forces[4 + k, c, near] + added[name, index]()
            for along in (1,) if axis == 0 else (-1, 1):
                for where, value in corner_share(k, name, index, along):
                    acc = acc + jnp.where(row == where, value, 0.0)
            b_at = head + 16 * (len(layers) + near)
            total = speed_in[k, at] + time_step * face_in[k, b_at : b_at + 16, :] * acc
            if axis == 0:
                u[c, (18 if upward else 0) + near] = total
            else:
                edge[k - 2, at] = total

    def late_share(k):
        upward = k == 1
        for index in (15,) if upward else (0, 1):
            for c in range(3):
                acc = forces[shelf[k], c, index - (14 if upward else 0), 0:8, :]
                u[c, 2 + index, 0:8, :] += time_step * buo[index, 0:8, :] * acc
        for name, index in speed_of_q if upward else speed_of_p:
            c = component[0][name]
            near = index if upward else index - 14
            acc = forces[shelf[4 + k], c, near, 0:8, :]
            for where, value in corner_share(k, name, index, -1):
                acc = acc + jnp.where(row[0:8] == where, value, 0.0)
            b_at = head + 16 * (len(stress_of_q if upward else stress_of_p) + near)
            u[c, (18 if upward else 0) + near, 0:8, :] += time_step * face_in[k, b_at : b_at + 8, :] * acc

    come(early)
    for k in (3, 1, 0):
        share(k)
    loads["lam"].wait()
    loads["mu"].wait()
    edge[0] = jnp.zeros((5, 16, 128), F32)
    planes(lambda x: stress_plane(u, st, lam, mu, edge, ns, x, 8))

    @pl.when(patient)
    def _():
        downward()

    come(late)
    for k in (1, 0):
        late_share(k)
    share(2)

    for (what, back), copy in copies.items():
        @pl.when(there(-back[0], -back[1]))
        def _():
            copy.wait_send()


def finish(u, st, lam, mu, edge, high, v_out, s_out, low, sem):
    copies = [
        pltpu.make_async_copy(u.at[:, 2:18], v_out, sem.at[4]),
        pltpu.make_async_copy(high.at[:, :, 8:16], s_out.at[:, :, 8:16], sem.at[5]),
    ]
    for copy in copies:
        copy.start()

    for part in range(4):
        cells = pl.ds(4 * part, 4)
        for x in range(4 * part, 4 * part + 4):
            stress_plane(u, st, lam, mu, edge, low, x, 0)
        copies.append(pltpu.make_async_copy(low.at[:, cells], s_out.at[:, cells, 0:8], sem.at[part]))
        copies[-1].start()
    for copy in copies:
        copy.wait()


def kept(*shape):
    return pltpu.VMEM(shape, F32)


def result(shape):
    return pltpu.HBM(shape, F32)


def local(velocity, stress, buoyancy, lame_lambda, shear_modulus, moment, signal, sx, sy, sz, count, *, nx, ny):
    hbm = pl.BlockSpec(memory_space=pltpu.HBM)
    on_chip = pl.BlockSpec(memory_space=pltpu.VMEM)
    vmem = pltpu.VMEM
    keep = functools.partial(pltpu.with_memory_space_constraint, memory_space=pltpu.VMEM)
    leave = functools.partial(pltpu.with_memory_space_constraint, memory_space=pltpu.HBM)
    args = (velocity, stress, buoyancy, lame_lambda, shear_modulus, jnp.transpose(moment, (0, 2, 1, 3)), signal, sx, sy, sz)
    done = pl.pallas_call(
        functools.partial(kernel, nx, ny),
        out_shape=(kept(3, 20, 16, 128), kept(6, 20, 16, 128), kept(16, 16, 128), kept(16, 16, 128), kept(2, 5, 16, 128), kept(6, 16, 16, 128)),
        in_specs=[hbm] * 10 + [pl.BlockSpec(memory_space=pltpu.SMEM)],
        out_specs=(on_chip,) * 6,
        scratch_shapes=[
            vmem((3, 16, 16, 128), F32),
            vmem((16, 16, 128), F32),
            vmem((1, 6, 1, 64), F32),
            vmem((1, 1, 64), F32),
            vmem((1, 1, 64), jnp.int32),
            vmem((1, 1, 64), jnp.int32),
            vmem((1, 1, 64), jnp.int32),
            vmem((3, 16, 16, 128), F32),
            vmem((12, 3, 2, 16, 128), F32),
            vmem((4, 120, 128), F32),
            vmem((4, 120, 128), F32),
            vmem((4, 5, 16, 128), F32),
            vmem((4, 5, 16, 128), F32),
            vmem((4, 24, 128), F32),
            vmem((4, 24, 128), F32),
            pltpu.SemaphoreType.DMA((18,)),
            pltpu.SemaphoreType.DMA((12,)),
            pltpu.SemaphoreType.DMA((12,)),
            pltpu.SemaphoreType.REGULAR,
        ],
        compiler_params=pltpu.CompilerParams(
            collective_id=0, has_side_effects=True, vmem_limit_bytes=48 * 1024 * 1024
        ),
        name="elastic_step",
    )(*map(leave, args), count)
    return pl.pallas_call(
        finish,
        out_shape=(result(velocity.shape), result(stress.shape)),
        in_specs=[on_chip] * 6,
        out_specs=(hbm, hbm),
        scratch_shapes=[vmem((6, 16, 8, 128), F32), pltpu.SemaphoreType.DMA((6,))],
        name="new_stress",
    )(*map(keep, done))


def solution(mesh):
    field = P(None, "gx", "gy", None)
    cells = P("gx", "gy", None)
    in_specs = (field, field, cells, cells, cells, P("gx", "gy", None, None)) + (cells,) * 5
    step = functools.partial(local, nx=mesh.shape["gx"], ny=mesh.shape["gy"])
    return jax.shard_map(step, mesh=mesh, in_specs=in_specs, out_specs=(field, field), check_vma=False)
```

```python
import functools
import jax
import jax.numpy as jnp
from jax import lax
from jax.sharding import PartitionSpec as P
import jax.experimental.pallas as pl
import jax.experimental.pallas.tpu as pltpu

MESH = pl.DeviceIdType.MESH
F32 = jnp.float32
BF16 = jnp.bfloat16

c1 = 9.0 / 8.0
c2 = -1.0 / 24.0
time_step = 0.1
d_table = (1.0, -27.0, 27.0, -1.0)
w_table = (-1.0, 9.0, 9.0, -1.0)
unscale = 1.0 / (16.0 * 16.0 * 24.0)
pairs = ((0, 3, 4), (3, 1, 5), (4, 5, 2))
neighbours = ((-1, -1), (-1, 0), (-1, 1), (0, -1), (0, 1), (1, -1), (1, 0), (1, 1))


stress_of_p = (("n", 15), ("t", 14), ("t", 15), ("r", 14), ("r", 15))
stress_of_q = (("n", 0), ("n", 1), ("t", 0), ("r", 0))
speed_of_p = (("n", 14), ("n", 15), ("t", 15), ("r", 15))
speed_of_q = (("n", 0), ("t", 0), ("t", 1), ("r", 0), ("r", 1))
component = ({"n": 0, "t": 1, "r": 2}, {"n": 1, "t": 0, "r": 2})
field = ({"n": 0, "t": 3, "r": 4}, {"n": 1, "t": 3, "r": 5})
role = tuple({c: r for r, c in names.items()} for names in component)
head = 8
early = ((0, 1), (1, 1), (-1, 1), (1, 0), (-1, 0))
late = ((1, -1), (-1, -1), (0, -1))


def give(get, upward):
    if upward:
        return {
            ("n", 0): lambda: -c2 * get("n", 15),
            ("t", 0): lambda: -c1 * get("t", 15) - c2 * get("t", 14),
            ("t", 1): lambda: -c2 * get("t", 15),
            ("r", 0): lambda: -c1 * get("r", 15) - c2 * get("r", 14),
            ("r", 1): lambda: -c2 * get("r", 15),
        }
    return {
        ("n", 14): lambda: c2 * get("n", 0),
        ("n", 15): lambda: c1 * get("n", 0) + c2 * get("n", 1),
        ("t", 15): lambda: c2 * get("t", 0),
        ("r", 15): lambda: c2 * get("r", 0),
    }


def corner_cells(sx, sy):
    cells = []
    for axis, (across, along) in enumerate(((sx, sy), (sy, sx))):
        other = 1 - axis
        for name, at in speed_of_p if across < 0 else speed_of_q:
            part = role[other][component[axis][name]]
            for what, index in stress_of_p if along < 0 else stress_of_q:
                if what == part:
                    cell = (field[other][what], at, index) if axis == 0 else (field[other][what], index, at)
                    if cell not in cells:
                        cells.append(cell)
    return cells


def lookup(offset, table):
    value = jnp.where(offset == 3, table[3], 0.0)
    for k in (2, 1, 0):
        value = jnp.where(offset == k, table[k], value)
    return value


def halves(low, high):
    lane = lax.broadcasted_iota(jnp.int32, (1, 128), 1)
    return jnp.where(lane < 64, low, high)


def stencil(length, start, position, table):
    cell = lax.broadcasted_iota(jnp.int32, (length, 128), 0) + start
    return lookup(cell - position + 1, table)


def unpack(rows):
    p = [rows[i : i + 1, :] for i in range(3)]
    mixed = [rows[3 + i : 4 + i, :] for i in range(3)]
    q = [halves(row, 0.0) for row in mixed]
    at = [halves(pltpu.roll(row, 64, 1), row).astype(jnp.int32) for row in mixed]
    return p, q, at


def depth_weights(pz):
    table = [halves(w, d) for w, d in zip(w_table, d_table)]
    weights = stencil(128, 0, pz, table).astype(BF16)
    return jnp.concatenate([weights, weights], axis=1)


def spread(tile, shift, pieces):
    p, q, (px, py, pz) = tile
    mixed = [halves(d, w) for w, d in zip(w_table, d_table)]
    position = (px + 16 * shift[0], py + 16 * shift[1])
    tables = ((mixed, w_table), (w_table, d_table))
    rows = []
    for axis, layers, start, count in pieces:
        one = [stencil(len(layers), layers[0], position[axis], table) for table in tables[axis]]
        two = [stencil(count, start, position[1 - axis], table) for table in tables[1 - axis]]
        for i in range(3):
            first, second = p[i] * one[0], q[i] * one[1]
            for k in range(len(layers)):
                rows.append(first[k : k + 1, :] * two[0] + second[k : k + 1, :] * two[1])
    value = jnp.concatenate(rows, axis=0)
    high = value.astype(BF16)
    low = (value - high.astype(F32)).astype(BF16)
    result = lax.dot_general(
        jnp.concatenate([high, low], axis=1), depth_weights(pz), (((1,), (1,)), ((), ())),
        preferred_element_type=F32,
    )
    parts, at = [], 0
    for axis, layers, start, count in pieces:
        size = 3 * len(layers) * count
        parts.append(result[at : at + size])
        at += size
    return parts


def diff(m2, m1, f, p1):
    return c1 * (f - m1) + c2 * (p1 - m2)


def along_y(f, low2, low1, high1, high2, forward):
    iy = lax.broadcasted_iota(jnp.int32, f.shape, 0)
    m1 = jnp.where(iy == 0, low1, pltpu.roll(f, 1, 0))
    p1 = jnp.where(iy == 15, high1, pltpu.roll(f, 15, 0))
    if forward:
        p2 = jnp.where(iy == 15, high2, jnp.where(iy == 14, high1, pltpu.roll(f, 14, 0)))
        return diff(m1, f, p1, p2)
    m2 = jnp.where(iy == 0, low2, jnp.where(iy == 1, low1, pltpu.roll(f, 2, 0)))
    return diff(m2, m1, f, p1)


def along_z(f, forward):
    iz = lax.broadcasted_iota(jnp.int32, f.shape, 1)
    m1 = jnp.where(iz < 1, 0.0, pltpu.roll(f, 1, 1))
    p1 = jnp.where(iz > 126, 0.0, pltpu.roll(f, 127, 1))
    if forward:
        p2 = jnp.where(iz > 125, 0.0, pltpu.roll(f, 126, 1))
        return diff(m1, f, p1, p2)
    m2 = jnp.where(iz < 2, 0.0, pltpu.roll(f, 2, 1))
    return diff(m2, m1, f, p1)


def stress_plane(u, st, lam, mu, edge, ns, x, rows):
    p = x + 2
    cells = pl.ds(rows, 8)

    def low(k):
        return edge[0, k, pl.ds(x, 1), :]

    def high(k):
        return edge[1, k, pl.ds(x, 1), :]

    def part(value):
        return value[rows : rows + 8]

    ux, uy, uz = u[0, p], u[1, p], u[2, p]
    exx = diff(u[0, p - 2, cells], u[0, p - 1, cells], part(ux), u[0, p + 1, cells])
    eyy = part(along_y(uy, low(0), low(1), high(0), None, False))
    ezz = along_z(part(uz), False)
    m = mu[x, cells]
    two = (2.0 * time_step) * m
    press = time_step * lam[x, cells] * (exx + eyy + ezz)
    shear = time_step * m
    ns[0, x, cells] = st[0, p, cells] + (press + two * exx)
    ns[1, x, cells] = st[1, p, cells] + (press + two * eyy)
    ns[2, x, cells] = st[2, p, cells] + (press + two * ezz)
    ns[3, x, cells] = st[3, p, cells] + shear * (
        part(along_y(ux, None, low(2), high(1), high(2), True))
        + diff(u[1, p - 1, cells], part(uy), u[1, p + 1, cells], u[1, p + 2, cells])
    )
    ns[4, x, cells] = st[4, p, cells] + shear * (
        along_z(part(ux), True) + diff(u[2, p - 1, cells], part(uz), u[2, p + 1, cells], u[2, p + 2, cells])
    )
    ns[5, x, cells] = st[5, p, cells] + shear * (
        along_z(part(uy), True) + part(along_y(uz, None, low(3), high(3), high(4), True))
    )


def planes(plane):
    def group(i, _):
        for k in range(4):
            plane(i * 4 + k)
        return 0

    lax.fori_loop(0, 4, group, 0)


def kernel(
    nx, ny,
    v_in, s_in, b_in, l_in, m_in, mom_in, sig_in, px_in, py_in, pz_in, cnt_in,
    u, st, lam, mu, edge, ns,
    vel, buo, mom, sig, px, py, pz,
    force, forces, face_out, face_in, speed_out, speed_in, corner_out, corner_in,
    load_sem, send_sem, recv_sem, ready,
):
    gx, gy = lax.axis_index("gx"), lax.axis_index("gy")

    def there(dx, dy):
        ok = True
        for at, step, count in ((gx, dx, nx), (gy, dy, ny)):
            if step:
                ok = ok & (at > 0) if step < 0 else ok & (at < count - 1)
        return ok

    barrier = pltpu.get_barrier_semaphore()
    expected, expected_below = 0, 0
    for dx, dy in neighbours:
        if dy >= 0:
            expected = expected + there(dx, dy).astype(jnp.int32)
        else:
            expected_below = expected_below + there(dx, dy).astype(jnp.int32)
        if dy <= 0:
            @pl.when(there(dx, dy))
            def _():
                pl.semaphore_signal(barrier, inc=1, device_id=(gx + dx, gy + dy), device_id_type=MESH)

    loads = {}
    for k, (name, src, dst) in enumerate((
        ("sxy", s_in.at[3, :, 8:16], st.at[3, 2:18, 8:16]), ("syy", s_in.at[1, :, 8:16], st.at[1, 2:18, 8:16]),
        ("syz", s_in.at[5, :, 8:16], st.at[5, 2:18, 8:16]),
        ("mom", mom_in, mom), ("sig", sig_in, sig), ("px", px_in, px), ("py", py_in, py),
        ("pz", pz_in, pz), ("sxx", s_in.at[0], st.at[0, 2:18]), ("sxz", s_in.at[4], st.at[4, 2:18]),
        ("buo", b_in, buo),
        ("sxy low", s_in.at[3, :, 0:8], st.at[3, 2:18, 0:8]), ("syy low", s_in.at[1, :, 0:8], st.at[1, 2:18, 0:8]),
        ("syz low", s_in.at[5, :, 0:8], st.at[5, 2:18, 0:8]), ("szz", s_in.at[2], st.at[2, 2:18]), ("vel", v_in, vel),
        ("lam", l_in, lam), ("mu", m_in, mu),
    )):
        loads[name] = pltpu.make_async_copy(src, dst, load_sem.at[k])
        loads[name].start()

    sides = ((-1, 0), (1, 0), (0, -1), (0, 1))
    corners = ((-1, -1), (-1, 1), (1, -1), (1, 1))
    lists = {n: corner_cells(*n) for n in corners}

    for f in (0, 3, 4):
        st[f, 0:2] = jnp.zeros((2, 16, 128), F32)
        st[f, 18:20] = jnp.zeros((2, 16, 128), F32)
    forces[...] = jnp.zeros((12, 3, 2, 16, 128), F32)
    for k, n in enumerate(sides):
        @pl.when(jnp.logical_not(there(*n)))
        def _():
            face_in[k] = jnp.zeros((88, 128), F32)
            speed_in[k] = jnp.zeros((7, 16, 128), F32)

    for k, n in enumerate(corners):
        @pl.when(jnp.logical_not(there(*n)))
        def _():
            corner_in[k] = jnp.zeros((24, 128), F32)

    pl.semaphore_wait(barrier, expected)
    for dx, dy in neighbours:
        if dy > 0:
            @pl.when(there(dx, dy))
            def _():
                pl.semaphore_signal(ready, inc=1, device_id=(gx + dx, gy + dy), device_id_type=MESH)

    for name in ("mom", "sig", "px", "py", "pz"):
        loads[name].wait()
    lane = lax.broadcasted_iota(jnp.int32, (1, 64), 1)
    live = (lane < cnt_in[0, 0, 0]).astype(F32)
    scaled = sig[0] * live * (-unscale)
    amp = [mom[0, r] * scaled for r in range(6)]
    rows = [jnp.concatenate([amp[pairs[i][0]], amp[pairs[i][2]]], axis=1) for i in range(3)]
    for i, ref in enumerate((px, py, pz)):
        rows.append(jnp.concatenate([amp[pairs[i][1]], ref[0].astype(F32)], axis=1))
    own_rows = jnp.concatenate(rows, axis=0)
    for k in range(4):
        face_out[k, 0:6, :] = own_rows
        face_out[k, 6:8, :] = jnp.zeros((2, 128), F32)
        corner_out[k, 0:6, :] = own_rows

    def remote(k, src, dst, n):
        return pltpu.make_async_remote_copy(
            src_ref=src, dst_ref=dst, send_sem=send_sem.at[k], recv_sem=recv_sem.at[k],
            device_id=(gx + n[0], gy + n[1]), device_id_type=MESH,
        )

    copies = {}
    for k, n in enumerate(sides):
        upward = k % 2 == 1
        size = head + 16 * len(stress_of_p if upward else stress_of_q)
        count = len(speed_of_p if upward else speed_of_q) + 2
        back = (-n[0], -n[1])
        copies["face", back] = remote(k, face_out.at[k, 0:size], face_in.at[k ^ 1, 0:size], n)
        copies["speed", back] = remote(4 + k, speed_out.at[k, 0:count], speed_in.at[k ^ 1, 0:count], n)
    for k, n in enumerate(corners):
        back = (-n[0], -n[1])
        size = -(-(6 + len(lists[back])) // 8) * 8
        copies["corner", back] = remote(8 + k, corner_out.at[k, 0:size], corner_in.at[3 - k, 0:size], n)

    def start(kind, towards):
        for k in towards:
            n = (corners if kind == "corner" else sides)[k]

            @pl.when(there(*n))
            def _():
                copies[kind, (-n[0], -n[1])].start()

    def arrive(kind, n):
        @pl.when(there(*n))
        def _():
            copies[kind, n].wait_recv()

    def layer(ref, axis, f, at):
        return ref[f, at + 2] if axis == 0 else ref[f, 2:18, at, :]

    def side_message(k):
        axis, upward = k // 2, k % 2 == 1
        at = head
        for name, index in stress_of_p if upward else stress_of_q:
            face_out[k, at : at + 16, :] = layer(st, axis, field[axis][name], index)
            at += 16

    def corner_message(k):
        cells = lists[-corners[k][0], -corners[k][1]]
        for r, (f, x, y) in enumerate(cells):
            corner_out[k, 6 + r : 7 + r, :] = st[f, 2 + x, y : y + 1, :]
        if 6 + len(cells) > 16:
            corner_out[k, 6 + len(cells) : 24, :] = jnp.zeros((18 - len(cells), 128), F32)

    for name in ("sxy", "syy", "syz"):
        loads[name].wait()
    side_message(3)
    for name in ("sxx", "sxz"):
        loads[name].wait()
    corner_message(1)
    corner_message(3)
    start("corner", (1, 3))
    start("face", (3,))
    for name in ("sxy low", "syy low", "syz low"):
        loads[name].wait()
    side_message(1)
    side_message(0)
    start("face", (1, 0))
    side_message(2)
    corner_message(0)
    corner_message(2)

    me = unpack(own_rows)
    force[...] = spread(me, (0, 0), [(0, tuple(range(16)), 0, 16)])[0].reshape(3, 16, 16, 128)

    loads["szz"].wait()
    loads["buo"].wait()
    loads["vel"].wait()

    def velocity_plane(x, rows):
        p = x + 2
        cells = pl.ds(rows, 8)

        def part(value):
            return value[rows : rows + 8]

        def share_y(f, at, forward):
            return part(along_y(st[f, at], 0.0, 0.0, 0.0, 0.0, forward))

        def share_z(f, at, forward):
            return along_z(st[f, at, cells], forward)

        ax = diff(st[0, p - 1, cells], st[0, p, cells], st[0, p + 1, cells], st[0, p + 2, cells])
        ax += share_y(3, p, False) + share_z(4, p, False)
        ay = diff(st[3, p - 2, cells], st[3, p - 1, cells], st[3, p, cells], st[3, p + 1, cells])
        ay += share_y(1, p, True) + share_z(5, p, False)
        az = diff(st[4, p - 2, cells], st[4, p - 1, cells], st[4, p, cells], st[4, p + 1, cells])
        az += share_y(5, p, False) + share_z(2, p, True)
        scale = time_step * buo[x, cells]
        u[0, p, cells] = vel[0, x, cells] + scale * (ax + force[0, x, cells])
        u[1, p, cells] = vel[1, x, cells] + scale * (ay + force[1, x, cells])
        u[2, p, cells] = vel[2, x, cells] + scale * (az + force[2, x, cells])

    def speed_message(k):
        axis, upward = k // 2, k % 2 == 1
        for at, (name, index) in enumerate(speed_of_p if upward else speed_of_q):
            speed_out[k, at] = layer(u, axis, component[axis][name], index)
        for at, index in enumerate((14, 15) if upward else (0, 1), at + 1):
            speed_out[k, at] = buo[index] if axis == 0 else buo[:, index, :]

    planes(lambda x: velocity_plane(x, 8))
    speed_message(3)
    start("speed", (3,))
    planes(lambda x: velocity_plane(x, 0))
    for k in (1, 0, 2):
        speed_message(k)
    start("speed", (1, 0))

    def downward():
        @pl.when(gy > 0)
        def _():
            pl.semaphore_wait(ready, expected_below)

        start("face", (2,))
        start("corner", (0, 2))
        start("speed", (2,))

    patient = gy == ny // 2

    @pl.when(jnp.logical_not(patient))
    def _():
        downward()

    def add_force(tile, n, pieces, shelf=None):
        parts = spread(tile, n, [piece for _, piece in pieces])
        for (region, (axis, layers, first, count)), part in zip(pieces, parts):
            base = {0: 0, 1: 14, 2: -2, 3: 16}[region % 2 + 2 * (region // 4)]
            region = (shelf or {}).get(region, region)
            at = 0
            for i in range(3):
                for a in layers:
                    forces[region, i, a - base, first : first + count, :] += part[at : at + count]
                    at += count

    every = (0, 16)
    block = {-1: (0, 8), 0: every, 1: (8, 8)}
    add_force(me, (0, 0), [
        (4, (0, (-1,), *every)), (5, (0, (16, 17), *every)), (6, (1, (-1,), *every)), (7, (1, (16, 17), *every)),
    ])
    low_in, high_in, low_out, high_out = (0, 1), (15,), (-2, -1), (16, 17)
    shelf = {0: 8, 1: 9, 4: 10, 5: 11}

    def tile_force(n):
        tx, ty = n
        if tx and ty:
            tile = unpack(corner_in[corners.index(n), 0:8, :])
        else:
            tile = unpack(face_in[sides.index(n), 0:8, :])
        pieces = []
        if tx:
            pieces.append((0 if tx < 0 else 1, (0, low_in if tx < 0 else high_in, *block[ty])))
            for sy in ((-1, 1) if ty == 0 else (ty,)):
                layers = (low_out if sy < 0 else high_out) if ty else ((-1,) if sy < 0 else (16, 17))
                pieces.append((6 if sy < 0 else 7, (1, layers, *block[tx])))
        else:
            pieces.append((2 if ty < 0 else 3, (1, low_in if ty < 0 else high_in, *every)))
        if ty:
            for sx in ((-1, 1) if tx == 0 else (tx,)):
                layers = (low_out if sx < 0 else high_out) if tx else ((-1,) if sx < 0 else (16, 17))
                pieces.append((4 if sx < 0 else 5, (0, layers, *block[ty])))
        add_force(tile, n, pieces, shelf if n in late else None)

    def come(tiles):
        for n in tiles:
            arrive("corner" if n[0] and n[1] else "face", n)
        for n in tiles:
            tile_force(n)

    def corner_share(k, name, index, along):
        axis = k // 2
        other = 1 - axis
        n = (sides[k][0] + (0 if axis == 0 else along), sides[k][1] + (along if axis == 0 else 0))

        def cell(what, where):
            key = (field[other][what], index, where) if axis == 0 else (field[other][what], where, index)
            r = 6 + lists[n].index(key)
            return corner_in[corners.index(n), r : r + 1, :]

        return [
            (where, value())
            for (what, where), value in give(cell, along < 0).items()
            if what == role[other][component[axis][name]]
        ]

    row = lax.broadcasted_iota(jnp.int32, (16, 128), 0)

    def share(k):
        axis, upward = k // 2, k % 2 == 1
        names = component[axis]
        layers = stress_of_q if upward else stress_of_p

        def mine(name, index):
            return layer(st, axis, field[axis][name], index)

        def theirs(name, index):
            at = head + 16 * layers.index((name, index))
            return face_in[k, at : at + 16, :]

        added = give(theirs, not upward)
        base = 14 if upward else 0
        for name in ("n", "t", "r"):
            c = names[name]
            for index in (base, base + 1):
                if upward and index == 14 and name != "n":
                    continue
                acc = forces[k, c, index - base]
                if (name, index) in added:
                    acc = acc + added[name, index]()
                if axis == 0:
                    u[c, 2 + index] += time_step * buo[index] * acc
                else:
                    u[c, 2:18, index, :] = u[c, 2:18, index, :] + time_step * buo[:, index, :] * acc
        arrive("speed", sides[k])
        added = give(mine, upward)
        for at, (name, index) in enumerate(speed_of_q if upward else speed_of_p):
            c = names[name]
            near = index if upward else index - 14
            acc = forces[4 + k, c, near] + added[name, index]()
            for along in (1,) if axis == 0 else (-1, 1):
                for where, value in corner_share(k, name, index, along):
                    acc = acc + jnp.where(row == where, value, 0.0)
            b_at = len(speed_of_q if upward else speed_of_p) + near
            total = speed_in[k, at] + time_step * speed_in[k, b_at] * acc
            if axis == 0:
                u[c, (18 if upward else 0) + near] = total
            else:
                edge[k - 2, at] = total

    def late_share(k):
        upward = k == 1
        for index in (15,) if upward else (0, 1):
            for c in range(3):
                acc = forces[shelf[k], c, index - (14 if upward else 0), 0:8, :]
                u[c, 2 + index, 0:8, :] += time_step * buo[index, 0:8, :] * acc
        for name, index in speed_of_q if upward else speed_of_p:
            c = component[0][name]
            near = index if upward else index - 14
            acc = forces[shelf[4 + k], c, near, 0:8, :]
            for where, value in corner_share(k, name, index, -1):
                acc = acc + jnp.where(row[0:8] == where, value, 0.0)
            b_at = len(speed_of_q if upward else speed_of_p) + near
            u[c, (18 if upward else 0) + near, 0:8, :] += time_step * speed_in[k, b_at, 0:8, :] * acc

    come(early)
    for k in (3, 1, 0):
        share(k)
    loads["lam"].wait()
    loads["mu"].wait()
    edge[0] = jnp.zeros((5, 16, 128), F32)
    planes(lambda x: stress_plane(u, st, lam, mu, edge, ns, x, 8))

    @pl.when(patient)
    def _():
        downward()

    come(late)
    for k in (1, 0):
        late_share(k)
    share(2)

    for (what, back), copy in copies.items():
        @pl.when(there(-back[0], -back[1]))
        def _():
            copy.wait_send()


def finish(u, st, lam, mu, edge, high, v_out, s_out, low, sem):
    copies = [
        pltpu.make_async_copy(u.at[:, 2:18], v_out, sem.at[4]),
        pltpu.make_async_copy(high.at[:, :, 8:16], s_out.at[:, :, 8:16], sem.at[5]),
    ]
    for copy in copies:
        copy.start()

    for part in range(4):
        cells = pl.ds(4 * part, 4)
        for x in range(4 * part, 4 * part + 4):
            stress_plane(u, st, lam, mu, edge, low, x, 0)
        copies.append(pltpu.make_async_copy(low.at[:, cells], s_out.at[:, cells, 0:8], sem.at[part]))
        copies[-1].start()
    for copy in copies:
        copy.wait()


def kept(*shape):
    return pltpu.VMEM(shape, F32)


def result(shape):
    return pltpu.HBM(shape, F32)


def local(velocity, stress, buoyancy, lame_lambda, shear_modulus, moment, signal, sx, sy, sz, count, *, nx, ny):
    hbm = pl.BlockSpec(memory_space=pltpu.HBM)
    on_chip = pl.BlockSpec(memory_space=pltpu.VMEM)
    vmem = pltpu.VMEM
    keep = functools.partial(pltpu.with_memory_space_constraint, memory_space=pltpu.VMEM)
    leave = functools.partial(pltpu.with_memory_space_constraint, memory_space=pltpu.HBM)
    args = (velocity, stress, buoyancy, lame_lambda, shear_modulus, jnp.transpose(moment, (0, 2, 1, 3)), signal, sx, sy, sz)
    done = pl.pallas_call(
        functools.partial(kernel, nx, ny),
        out_shape=(kept(3, 20, 16, 128), kept(6, 20, 16, 128), kept(16, 16, 128), kept(16, 16, 128), kept(2, 5, 16, 128), kept(6, 16, 16, 128)),
        in_specs=[hbm] * 10 + [pl.BlockSpec(memory_space=pltpu.SMEM)],
        out_specs=(on_chip,) * 6,
        scratch_shapes=[
            vmem((3, 16, 16, 128), F32),
            vmem((16, 16, 128), F32),
            vmem((1, 6, 1, 64), F32),
            vmem((1, 1, 64), F32),
            vmem((1, 1, 64), jnp.int32),
            vmem((1, 1, 64), jnp.int32),
            vmem((1, 1, 64), jnp.int32),
            vmem((3, 16, 16, 128), F32),
            vmem((12, 3, 2, 16, 128), F32),
            vmem((4, 88, 128), F32),
            vmem((4, 88, 128), F32),
            vmem((4, 7, 16, 128), F32),
            vmem((4, 7, 16, 128), F32),
            vmem((4, 24, 128), F32),
            vmem((4, 24, 128), F32),
            pltpu.SemaphoreType.DMA((18,)),
            pltpu.SemaphoreType.DMA((12,)),
            pltpu.SemaphoreType.DMA((12,)),
            pltpu.SemaphoreType.REGULAR,
        ],
        compiler_params=pltpu.CompilerParams(
            collective_id=0, has_side_effects=True, vmem_limit_bytes=48 * 1024 * 1024
        ),
        name="elastic_step",
    )(*map(leave, args), count)
    return pl.pallas_call(
        finish,
        out_shape=(result(velocity.shape), result(stress.shape)),
        in_specs=[on_chip] * 6,
        out_specs=(hbm, hbm),
        scratch_shapes=[vmem((6, 16, 8, 128), F32), pltpu.SemaphoreType.DMA((6,))],
        name="new_stress",
    )(*map(keep, done))


def solution(mesh):
    field = P(None, "gx", "gy", None)
    cells = P("gx", "gy", None)
    in_specs = (field, field, cells, cells, cells, P("gx", "gy", None, None)) + (cells,) * 5
    step = functools.partial(local, nx=mesh.shape["gx"], ny=mesh.shape["gy"])
    return jax.shard_map(step, mesh=mesh, in_specs=in_specs, out_specs=(field, field), check_vma=False)
```
